256 devices in a mesh: pair: 64 (over x, z, core), fock: 4 (over y).
Axes of the slice: x: 4, y: 4, z: 8, core: 2. Of those that a mesh axis runs over, the one named last changes fastest.
Arguments:
- three_center: bfloat16 [3072, 64, 4096], P('pair', 'fock'), may hold values from -0.75 to 0.75
- coefficients: bfloat16 [32, 19968], replicated, may hold values from -0.23925781 to 0.23925781
- metric_inv: bfloat16 [512, 512], replicated, as said below
- target_owner: int32 [3072, 1], P('pair'), may hold values from 0 to 63; in each aligned block of 48 rows (0 to 47, 48 to 95, ...) at most 2 rows name the same one
- row_slot: int32 [3072], P('pair'), may hold values from 0 to 7
- aux_block: int32 [3072], P('pair'), may hold values from 0 to 7
- ao_block: int32 [3072], P('pair'), may hold values from 0 to 311
Outputs:
- exchange: bfloat16 [32768, 512], P(('pair', 'fock'))
The draws below stay inside these ranges and needn't reach their ends.
Inputs may be any that keep to these rules, and one draw needn't show every extreme that they name: `target_owner`: among the 48 blocks of one index of pair, no owner is named more than 2 times; some owner is named exactly 2 times. `metric_inv`: symmetric.
All inputs are finite; a program needn't handle non-finite values.
Results may differ from the reference program's by a relative error of at most 0.0033.
Values may be sent and summed in bfloat16 or wider, within the bound.
No kernel may reach another device: no remote copies, remote signals or barrier semaphores. Data moves between devices by JAX's collectives and lax.ppermute only.
A program may use at most 128 MiB of HBM per device.

```python
import math
import jax
import jax.numpy as jnp
import numpy as np
from jax import lax

BLK = 64
AUXB = 8
AOB = 312
OCC = 32
ROWB = 8
TRIP_DEV = 48
NAUX = 512
NAO = 19968
CAP = 2
TRIPS = 3072
N_PAIR = 64


def draw_metric_inv(key, part):
    key = jax.random.fold_in(key, 5)
    first, second = jax.random.split(key)
    spread = 0.02 * jax.random.normal(first, (NAUX, NAUX), jnp.float32)
    diagonal = jnp.exp(jax.random.uniform(second, (NAUX,), jnp.float32, -0.7, 1.4))
    symmetric = 0.5 * (spread + spread.T)
    return (symmetric + jnp.diag(diagonal)).astype(jnp.bfloat16)


def touch_ends(array, stream_key, least, top_value):
    longest = array.shape.index(max(array.shape))
    spots = []
    for shift in (0, 1):
        where = [jax.random.randint(jax.random.fold_in(stream_key, axis), (), 0, length) for axis, length in enumerate(array.shape)]
        where[longest] = (where[longest] + shift) % array.shape[longest]
        spots.append(tuple(where))
    return array.at[spots[0]].set(least).at[spots[1]].set(top_value)


def shard_levels(stream_key, shape, shards, low, largest):
    level = 1.0
    for dim, blocks in shards:
        draws = jax.random.uniform(jax.random.fold_in(jax.random.fold_in(stream_key, 6), dim), (blocks,), jnp.float32, low / len(shards), largest / len(shards))
        level = level * jnp.repeat(jnp.exp(draws), shape[dim] // blocks).reshape((-1,) + (1,) * (len(shape) - 1 - dim))
    return level


def deal_out(key, own, number, rows, count, top, most, slope):
    sequence = jax.random.permutation(key, count)
    crowded, common = load_shares(count, rows * top, most, slope, True), load_shares(count, rows * top, most, slope, False)
    places = jnp.arange(count)

    def named(lengths, turn):
        used = int((lengths > 0).sum())
        fixed = max(1, used // 4)
        passed = fixed + (places - fixed + turn * (used - fixed)) % max(1, count - fixed)
        return jnp.zeros((count,), jnp.int32).at[sequence[jnp.where(places < fixed, places, passed)]].set(jnp.asarray(lengths, jnp.int32))

    lengths = jnp.where(number % 4 == 0, named(crowded, number // 4), named(common, number - number // 4 - 1))
    mixed = jax.random.permutation(jax.random.fold_in(own, 3), count)
    donor, taker = mixed[0:count // 2 * 2:2], mixed[1:count // 2 * 2:2]
    slack = jnp.minimum(lengths[donor] - 1, most - lengths[taker]) // 2
    slack = jnp.where((donor == sequence[0]) | (taker == sequence[0]) | (lengths[taker] == 0), 0, jnp.maximum(slack, 0))
    passed = jax.random.randint(jax.random.fold_in(own, 4), (count // 2,), 0, 1 << 20) % (slack + 1)
    lengths = lengths.at[donor].add(-passed).at[taker].add(passed)
    items = jnp.searchsorted(jnp.cumsum(lengths), jnp.arange(rows * top), side="right").astype(jnp.int32)
    table = items.reshape(top, rows).T
    table = table[jax.random.permutation(jax.random.fold_in(own, 1), rows)]
    turn = jax.random.randint(jax.random.fold_in(own, 2), (rows, 1), 0, top)
    return jnp.take_along_axis(table, (jnp.arange(top)[None, :] + turn) % top, axis=1)


def load_shares(number_of, total, limit, skew, full):
    portions = [(1 << 20) // math.isqrt(rank ** skew) + 1 for rank in range(1, number_of + 1)]
    largest = limit if full else min(limit, max(-(-total // number_of), total * portions[0] // sum(portions)))
    least = 1 if total - largest >= number_of - 1 else 0
    holding, spare = [largest] + [least] * (number_of - 1), total - largest - least * (number_of - 1)
    while spare > 0:
        movable = [i for i in range(1, number_of) if holding[i] < largest] or [i for i in range(1, number_of) if holding[i] < limit]
        whole, budget = sum([portions[i] for i in movable]), spare
        for i in movable:
            more = min(limit - holding[i], max(1, budget * portions[i] // whole), spare)
            holding[i] = holding[i] + more
            spare = spare - more
    return np.array(holding)


def scatter_about(stream_key, extent, scale, reach, cuts=(), held_as=jnp.bfloat16):
    drawn = jax.random.normal(stream_key, extent, jnp.float32) * scale
    if len(cuts) > 0:
        drawn = shard_levels(stream_key, extent, cuts, -0.22, 0.18) * drawn
    return jnp.clip(drawn, min=-reach, max=reach).astype(held_as)


def setup_inputs(seed: int = 0) -> dict:
    splits = jax.random.split(jax.random.key(seed), 8)
    three_center = scatter_about(splits[0], (TRIPS, BLK, BLK * BLK), BLK ** -0.5, 0.75, ((0, 64), (1, 4)))
    coefficients = scatter_about(splits[1], (OCC, NAO), 0.04, 0.23925781)
    metric_inv = draw_metric_inv(jax.random.fold_in(splits[7], 71), 0)
    target_owner_keys = jax.random.split(jax.random.fold_in(splits[3], 1), TRIPS // TRIP_DEV)
    target_owner_turns = jax.random.permutation(jax.random.fold_in(splits[3], 3), TRIPS // TRIP_DEV)
    target_owner = jax.vmap(lambda own, number: deal_out(jax.random.fold_in(splits[3], 2), own, number, TRIP_DEV, N_PAIR, 1, CAP, 2))(target_owner_keys, target_owner_turns).reshape((TRIPS, 1))
    row_slot = touch_ends(jax.random.randint(splits[4], (TRIPS,), 0, ROWB), jax.random.fold_in(splits[4], 1), 0, ROWB - 1).astype(jnp.int32)
    aux_block = touch_ends(jax.random.randint(splits[5], (TRIPS,), 0, AUXB), jax.random.fold_in(splits[5], 1), 0, AUXB - 1).astype(jnp.int32)
    ao_block = touch_ends(jax.random.randint(splits[6], (TRIPS,), 0, AOB), jax.random.fold_in(splits[6], 1), 0, AOB - 1).astype(jnp.int32)
    return dict(three_center=three_center, coefficients=coefficients, metric_inv=metric_inv, target_owner=target_owner, row_slot=row_slot, aux_block=aux_block, ao_block=ao_block)


def reference(three_center, coefficients, metric_inv, target_owner, row_slot, aux_block, ao_block):
    trip_count = three_center.shape[0]
    coef_blocks = coefficients.reshape(OCC, AOB, BLK).astype(jnp.float32)
    tensor_all = three_center.reshape(N_PAIR, TRIP_DEV, BLK, BLK, BLK)
    lblocks_all = ao_block.reshape(N_PAIR, TRIP_DEV)

    def make_units(packed):
        tensor, lblocks = packed
        picked = jnp.take(coef_blocks, lblocks, axis=1)
        made = jnp.einsum('tmlp,itl->tmip', tensor.astype(jnp.float32), picked)
        return made.astype(jnp.bfloat16)

    units = lax.map(make_units, (tensor_all, lblocks_all))
    units = units.reshape(trip_count, BLK * OCC * BLK)
    target = target_owner[:, 0].astype(jnp.int32)
    combo = (row_slot * AUXB + aux_block).astype(jnp.int32)
    ordering = jnp.argsort(target, stable=True).astype(jnp.int32)
    owners = jnp.arange(N_PAIR, dtype=jnp.int32)
    counts = jnp.sum((target[None, :] == owners[:, None]).astype(jnp.int32), axis=1)
    starts = jnp.cumsum(counts) - counts
    most_in = N_PAIR * CAP
    width = ROWB * BLK

    def per_owner(owner):
        start = starts[owner]
        count = counts[owner]
        offsets = jnp.arange(most_in, dtype=jnp.int32)
        valid = offsets < count
        position = jnp.clip(start + offsets, 0, trip_count - 1)
        chosen = ordering[position]
        rows = units[chosen].astype(jnp.float32)
        segment = jnp.where(valid, combo[chosen], ROWB * AUXB)
        summed = jax.ops.segment_sum(rows, segment, ROWB * AUXB + 1)[:ROWB * AUXB]
        gathered = summed.astype(jnp.bfloat16).reshape(ROWB, AUXB, BLK, OCC, BLK)
        gathered = gathered.transpose(0, 2, 3, 1, 4).reshape(width * OCC, NAUX)
        fitted = jnp.dot(gathered, metric_inv, preferred_element_type=jnp.float32).astype(jnp.bfloat16)
        left = fitted.reshape(width, OCC * NAUX)
        right = gathered.reshape(width, OCC * NAUX)
        return jnp.dot(left, right.T, preferred_element_type=jnp.float32).astype(jnp.bfloat16)

    blocks = lax.map(per_owner, owners)
    return blocks.reshape(N_PAIR * width, width)
```

```python
import functools

import jax
import jax.numpy as jnp
from jax import lax
from jax.experimental import pallas as pl
from jax.experimental.pallas import tpu as pltpu
from jax.sharding import Mesh, PartitionSpec as P

BLK = 64
AUXB = 8
ROWB = 8
NAUX = 512
LANES = 128
SLOTS = 4
AXES = ("x", "z", "c", "y")


def units_kernel(ao_ref, chip_ref, slot_ref, three_ref, coef_ref, spread_ref, out_ref):
    step = pl.program_id(0)
    half = ao_ref[step] % 2
    rows = three_ref[0].astype(jnp.float32)
    tiles = rows.shape[1] // LANES
    stacked = [
        jnp.concatenate([rows[h * 8 : h * 8 + 8, j * LANES : (j + 1) * LANES] for j in range(tiles)], axis=0)
        for h in range(2)
    ]
    right = jnp.concatenate(stacked, axis=1).astype(jnp.bfloat16)
    depth = tiles * 8
    orbitals = coef_ref.shape[0]
    spread = jnp.dot(coef_ref[...], spread_ref[half], preferred_element_type=jnp.float32)
    lane = lax.broadcasted_iota(jnp.int32, (orbitals, 8, depth), 2)
    row = lax.broadcasted_iota(jnp.int32, (orbitals, 8, depth), 1)
    keep = (lane % 8) == row
    parts = []
    for parity in range(2):
        wide = jnp.broadcast_to(spread[:, None, parity * depth : (parity + 1) * depth], (orbitals, 8, depth))
        left = jnp.where(keep, wide, 0.0).reshape(orbitals * 8, depth).astype(jnp.bfloat16)
        made = jnp.dot(left, right, preferred_element_type=jnp.float32)
        parts.append(made.reshape(orbitals // 2, 2, 8, 2 * LANES))
    low = lax.broadcasted_iota(jnp.int32, (orbitals // 2, 8, LANES), 2) < BLK
    done = []
    for h in range(2):
        cut = slice(h * LANES, (h + 1) * LANES)
        stay = jnp.where(low, parts[0][:, 0, :, cut], parts[1][:, 1, :, cut])
        move = jnp.where(low, parts[0][:, 1, :, cut], parts[1][:, 0, :, cut])
        done.append(stay + pltpu.roll(move, BLK, 2))
    units = jnp.stack(done, axis=1).reshape(orbitals * 8, LANES).astype(jnp.bfloat16)
    out_ref[0, :, 0] = units.reshape(8, orbitals, LANES)


def make_units(three_center, coefficients, ao_block, chip, slot, chips):
    count, rows, depth = three_center.shape
    orbitals = coefficients.shape[0]
    wide = BLK // 2 * 8
    held = jnp.arange(LANES)[None, :, None]
    column = jnp.arange(2 * wide)[None, None, :]
    half = jnp.arange(2)[:, None, None]
    spread = (held == half * BLK + 2 * (column % wide // 8) + column // wide).astype(jnp.bfloat16)
    grid_spec = pltpu.PrefetchScalarGridSpec(
        num_scalar_prefetch=3,
        grid=(count,),
        in_specs=[
            pl.BlockSpec((1, rows, depth), lambda t, ao, chip, slot: (t, 0, 0)),
            pl.BlockSpec((orbitals, LANES), lambda t, ao, chip, slot: (0, ao[t] // 2)),
            pl.BlockSpec((2, LANES, 2 * wide), lambda t, ao, chip, slot: (0, 0, 0)),
        ],
        out_specs=pl.BlockSpec((1, 8, 1, orbitals, LANES), lambda t, ao, chip, slot: (chip[t], 0, slot[t], 0, 0)),
    )
    return pl.pallas_call(
        units_kernel,
        grid_spec=grid_spec,
        out_shape=jax.ShapeDtypeStruct((chips, 8, SLOTS, orbitals, LANES), jnp.bfloat16),
        name="units",
    )(ao_block, chip, slot, three_center, coefficients, spread)


def exchange_kernel(tag_ref, in_ref, metric_ref, out_ref, total, fitted):
    step = pl.program_id(0)
    sources, quarters, slots = in_ref.shape[0], in_ref.shape[1], in_ref.shape[2]

    @pl.when(step == 0)
    def _():
        total[...] = jnp.zeros_like(total)

    def add(k, carry):
        source, slot = k // slots, k % slots
        tag = tag_ref[step * sources + source, slot]

        @pl.when(tag >= 0)
        def _():
            owner, row, aux = tag // (ROWB * AUXB), tag // AUXB % ROWB, tag % AUXB
            for quarter in range(quarters):
                start = pl.multiple_of(row * BLK + quarter * 16, 16)
                for pair in range(2):
                    place = (owner, pair, aux, pl.ds(start, 16), slice(None))
                    total[place] += in_ref[source, quarter, slot, pair * 16 : pair * 16 + 16, :].astype(jnp.float32)

        return carry

    lax.fori_loop(0, sources * slots, add, 0)

    @pl.when(step == pl.num_programs(0) - 1)
    def _():
        for owner in range(2):
            for pair in range(2):
                whole = jnp.concatenate(
                    [total[owner, pair, aux].astype(jnp.bfloat16) for aux in range(AUXB)], axis=1
                )
                fitted[...] = jnp.dot(whole, metric_ref[...], preferred_element_type=jnp.float32).astype(jnp.bfloat16)
                part = lax.dot_general(
                    fitted[...], whole, (((1,), (1,)), ((), ())), preferred_element_type=jnp.float32
                )
                if pair == 0:
                    out_ref[owner] = part
                else:
                    out_ref[owner] += part


def make_exchange(tags, incoming, metric):
    sources, quarters, slots, rows, lanes = incoming.shape
    step = 4
    width = ROWB * BLK
    grid_spec = pltpu.PrefetchScalarGridSpec(
        num_scalar_prefetch=1,
        grid=(sources // step,),
        in_specs=[
            pl.BlockSpec((step, quarters, slots, rows, lanes), lambda s, tags: (s, 0, 0, 0, 0)),
            pl.BlockSpec(metric.shape, lambda s, tags: (0, 0)),
        ],
        out_specs=pl.BlockSpec((2, width, width), lambda s, tags: (0, 0, 0)),
        scratch_shapes=[
            pltpu.VMEM((2, 2, AUXB, width, lanes), jnp.float32),
            pltpu.VMEM((width, AUXB * lanes), jnp.bfloat16),
        ],
    )
    return pl.pallas_call(
        exchange_kernel,
        grid_spec=grid_spec,
        out_shape=jax.ShapeDtypeStruct((2, width, width), jnp.float32),
        compiler_params=pltpu.CompilerParams(vmem_limit_bytes=48 * 1024 * 1024),
        name="exchange",
    )(tags, incoming, metric)


def double_metric(metric_inv):
    blocks = metric_inv.reshape(AUXB, 1, BLK, AUXB, 1, BLK)
    same = jnp.eye(2, dtype=jnp.bool_).reshape(1, 2, 1, 1, 2, 1)
    return jnp.where(same, blocks, 0).reshape(2 * NAUX, 2 * NAUX)


def body(three_center, coefficients, metric_inv, target_owner, row_slot, aux_block, ao_block):
    count, rows, depth = three_center.shape
    orbitals = coefficients.shape[0]
    cores = lax.axis_size("c")
    chips = lax.axis_size("x") * lax.axis_size("z")
    target = target_owner[:, 0]
    chip, core = target // cores, target % cores
    code = core * (ROWB * AUXB) + row_slot * AUXB + aux_block
    counter = jnp.arange(count, dtype=jnp.int32)
    earlier = (chip[:, None] == chip[None, :]) & (counter[None, :] < counter[:, None])
    slot = jnp.sum(earlier.astype(jnp.int32), axis=1)
    placed = (jnp.arange(chips * SLOTS, dtype=jnp.int32)[:, None] == (chip * SLOTS + slot)[None, :])
    tags = jnp.max(jnp.where(placed, code[None, :], -1), axis=1).reshape(chips, 1, SLOTS)
    tags = jnp.broadcast_to(tags, (chips, cores, SLOTS)).reshape(chips * cores, SLOTS)
    tags = lax.all_to_all(tags, ("x", "z", "c"), split_axis=0, concat_axis=0, tiled=True)
    outgoing = make_units(three_center, coefficients, ao_block, chip, slot, chips)
    outgoing = outgoing.reshape(chips * 8, SLOTS, orbitals, LANES)
    incoming = lax.all_to_all(outgoing, AXES, split_axis=0, concat_axis=0, tiled=True)
    incoming = incoming.reshape(chips * cores, 4, SLOTS, orbitals, LANES)
    partial = make_exchange(tags, incoming, double_metric(metric_inv))
    width = ROWB * BLK
    share = width // 4
    partial = partial.reshape(cores * 4, share, width)
    partial = lax.all_to_all(partial, ("c", "y"), split_axis=0, concat_axis=0, tiled=True)
    return jnp.sum(partial, axis=0).astype(jnp.bfloat16)


def solution(mesh):
    split = Mesh(mesh.devices.reshape(4, 8, 2, 4), AXES)
    pair = ("x", "z", "c")
    in_specs = (P(pair, "y", None), P(), P(), P(pair, None), P(pair), P(pair), P(pair))
    out_specs = P(AXES, None)
    return jax.shard_map(body, mesh=split, in_specs=in_specs, out_specs=out_specs, check_vma=False)
```

```python
import functools

import jax
import jax.numpy as jnp
from jax import lax
from jax.experimental import pallas as pl
from jax.experimental.pallas import tpu as pltpu
from jax.sharding import Mesh, PartitionSpec as P

BLK = 64
AUXB = 8
ROWB = 8
NAUX = 512
LANES = 128
SLOTS = 4
AXES = ("x", "z", "c", "y")


def units_kernel(ao_ref, chip_ref, slot_ref, three_ref, coef_ref, spread_ref, out_ref, made_ref, sems):
    step = pl.program_id(0)
    group, _, depth_in = three_ref.shape
    tiles = depth_in // LANES
    depth = tiles * 8
    orbitals = coef_ref.shape[0]
    lane = lax.broadcasted_iota(jnp.int32, (orbitals, 8, depth), 2)
    row = lax.broadcasted_iota(jnp.int32, (orbitals, 8, depth), 1)
    keep = (lane % 8) == row
    low = lax.broadcasted_iota(jnp.int32, (orbitals // 2, 8, LANES), 2) < BLK

    def copy(unit):
        return pltpu.make_async_copy(
            made_ref.at[unit], out_ref.at[chip_ref[unit], :, slot_ref[unit]], sems.at[unit]
        )

    for k in range(group):
        unit = step * group + k
        ao = ao_ref[unit]
        rows = three_ref[k].astype(jnp.float32)
        stacked = [
            jnp.concatenate([rows[h * 8 : h * 8 + 8, j * LANES : (j + 1) * LANES] for j in range(tiles)], axis=0)
            for h in range(2)
        ]
        right = jnp.concatenate(stacked, axis=1).astype(jnp.bfloat16)
        picked = coef_ref[:, pl.ds(pl.multiple_of(ao // 2 * LANES, LANES), LANES)]
        spread = jnp.dot(picked, spread_ref[ao % 2], preferred_element_type=jnp.float32)
        parts = []
        for parity in range(2):
            wide = jnp.broadcast_to(spread[:, None, parity * depth : (parity + 1) * depth], (orbitals, 8, depth))
            left = jnp.where(keep, wide, 0.0).reshape(orbitals * 8, depth).astype(jnp.bfloat16)
            made = jnp.dot(left, right, preferred_element_type=jnp.float32)
            parts.append(made.reshape(orbitals // 2, 2, 8, 2 * LANES))
        done = []
        for h in range(2):
            cut = slice(h * LANES, (h + 1) * LANES)
            stay = jnp.where(low, parts[0][:, 0, :, cut], parts[1][:, 1, :, cut])
            move = jnp.where(low, parts[0][:, 1, :, cut], parts[1][:, 0, :, cut])
            done.append(stay + pltpu.roll(move, BLK, 2))
        units = jnp.stack(done, axis=1).reshape(orbitals * 8, LANES).astype(jnp.bfloat16)
        made_ref[unit] = units.reshape(8, orbitals, LANES)
        copy(unit).start()

    @pl.when(step == pl.num_programs(0) - 1)
    def _():
        for unit in range(made_ref.shape[0]):
            copy(unit).wait()


def make_units(three_center, coefficients, ao_block, chip, slot, chips):
    count, rows, depth = three_center.shape
    orbitals, functions = coefficients.shape
    wide = BLK // 2 * 8
    held = jnp.arange(LANES)[None, :, None]
    column = jnp.arange(2 * wide)[None, None, :]
    half = jnp.arange(2)[:, None, None]
    spread = (held == half * BLK + 2 * (column % wide // 8) + column // wide).astype(jnp.bfloat16)
    group = 4
    grid_spec = pltpu.PrefetchScalarGridSpec(
        num_scalar_prefetch=3,
        grid=(count // group,),
        in_specs=[
            pl.BlockSpec((group, rows, depth), lambda t, ao, chip, slot: (t, 0, 0)),
            pl.BlockSpec((orbitals, functions), lambda t, ao, chip, slot: (0, 0)),
            pl.BlockSpec((2, LANES, 2 * wide), lambda t, ao, chip, slot: (0, 0, 0)),
        ],
        out_specs=pl.BlockSpec(memory_space=pl.ANY),
        scratch_shapes=[
            pltpu.VMEM((count, 8, orbitals, LANES), jnp.bfloat16),
            pltpu.SemaphoreType.DMA((count,)),
        ],
    )
    return pl.pallas_call(
        units_kernel,
        grid_spec=grid_spec,
        out_shape=jax.ShapeDtypeStruct((chips, 8, SLOTS, orbitals, LANES), jnp.bfloat16),
        compiler_params=pltpu.CompilerParams(vmem_limit_bytes=32 * 1024 * 1024),
        name="units",
    )(ao_block, chip, slot, three_center, coefficients, spread)


def own_exchange(whole, metric_ref, fitted, out_ref, first):
    fitted[...] = jnp.dot(whole, metric_ref[...], preferred_element_type=jnp.float32).astype(jnp.bfloat16)
    part = lax.dot_general(fitted[...], whole, (((1,), (1,)), ((), ())), preferred_element_type=jnp.float32)
    if first:
        out_ref[...] = part
    else:
        out_ref[...] += part


def gather_kernel(tag_ref, core_ref, in_ref, metric_ref, mine_ref, out_ref, total, fitted):
    step = pl.program_id(0)
    sources, quarters, slots = in_ref.shape[0], in_ref.shape[1], in_ref.shape[2]

    @pl.when(step == 0)
    def _():
        total[...] = jnp.zeros_like(total)

    def add(k, carry):
        source, slot = k // slots, k % slots
        tag = tag_ref[step * sources + source, slot]

        @pl.when(tag >= 0)
        def _():
            owner, row, aux = tag // (ROWB * AUXB), tag // AUXB % ROWB, tag % AUXB
            places = [
                (owner, pair, aux, pl.ds(pl.multiple_of(row * BLK + quarter * 16, 16), 16), slice(None))
                for quarter in range(quarters)
                for pair in range(2)
            ]
            news = [
                in_ref[source, quarter, slot, pair * 16 : pair * 16 + 16, :].astype(jnp.float32)
                for quarter in range(quarters)
                for pair in range(2)
            ]
            sums = [total[place] + new for place, new in zip(places, news)]
            for place, value in zip(places, sums):
                total[place] = value

        return carry

    lax.fori_loop(0, sources * slots, add, 0)

    @pl.when(step == pl.num_programs(0) - 1)
    def _():
        mine = core_ref[0]
        for pair in range(2):
            whole = [total[1 - mine, pair, aux].astype(jnp.bfloat16) for aux in range(AUXB)]
            own_exchange(jnp.concatenate(whole, axis=1), metric_ref, fitted, out_ref, pair == 0)
        for pair in range(2):
            for aux in range(AUXB):
                mine_ref[pair, :, aux * LANES : (aux + 1) * LANES] = total[mine, pair, aux].astype(jnp.bfloat16)


def rest_kernel(mine_ref, metric_ref, out_ref, fitted):
    for pair in range(2):
        own_exchange(mine_ref[pair], metric_ref, fitted, out_ref, pair == 0)


def make_exchange(tags, core, incoming, metric):
    sources, quarters, slots, rows, lanes = incoming.shape
    step = 16
    width = ROWB * BLK
    inner = AUXB * lanes
    grid_spec = pltpu.PrefetchScalarGridSpec(
        num_scalar_prefetch=2,
        grid=(sources // step,),
        in_specs=[
            pl.BlockSpec((step, quarters, slots, rows, lanes), lambda s, tags, core: (s, 0, 0, 0, 0)),
            pl.BlockSpec(metric.shape, lambda s, tags, core: (0, 0)),
        ],
        out_specs=[
            pl.BlockSpec((2, width, inner), lambda s, tags, core: (0, 0, 0)),
            pl.BlockSpec((width, width), lambda s, tags, core: (0, 0)),
        ],
        scratch_shapes=[
            pltpu.VMEM((2, 2, AUXB, width, lanes), jnp.float32),
            pltpu.VMEM((width, inner), jnp.bfloat16),
        ],
    )
    params = pltpu.CompilerParams(vmem_limit_bytes=48 * 1024 * 1024)
    mine, sent = pl.pallas_call(
        gather_kernel,
        grid_spec=grid_spec,
        out_shape=[
            jax.ShapeDtypeStruct((2, width, inner), jnp.bfloat16),
            jax.ShapeDtypeStruct((width, width), jnp.float32),
        ],
        compiler_params=params,
        name="gather_exchange",
    )(tags, core, incoming, metric)
    got = lax.ppermute(sent, "c", [(0, 1), (1, 0)])
    flops = 4 * width * inner * (inner + width)
    held = pl.pallas_call(
        rest_kernel,
        out_shape=jax.ShapeDtypeStruct((width, width), jnp.float32),
        scratch_shapes=[pltpu.VMEM((width, inner), jnp.bfloat16)],
        compiler_params=params,
        cost_estimate=pl.CostEstimate(flops=flops, bytes_accessed=5 * width * inner * 2, transcendentals=0),
        name="own_exchange",
    )(mine, metric)
    return held + got


def double_metric(metric_inv):
    blocks = metric_inv.reshape(AUXB, 1, BLK, AUXB, 1, BLK)
    same = jnp.eye(2, dtype=jnp.bool_).reshape(1, 2, 1, 1, 2, 1)
    return jnp.where(same, blocks, 0).reshape(2 * NAUX, 2 * NAUX)


def body(three_center, coefficients, metric_inv, target_owner, row_slot, aux_block, ao_block):
    count, rows, depth = three_center.shape
    orbitals = coefficients.shape[0]
    cores = lax.axis_size("c")
    chips = lax.axis_size("x") * lax.axis_size("z")
    target = target_owner[:, 0]
    chip, core = target // cores, target % cores
    code = core * (ROWB * AUXB) + row_slot * AUXB + aux_block
    counter = jnp.arange(count, dtype=jnp.int32)
    earlier = (chip[:, None] == chip[None, :]) & (counter[None, :] < counter[:, None])
    slot = jnp.sum(earlier.astype(jnp.int32), axis=1)
    placed = (jnp.arange(chips * SLOTS, dtype=jnp.int32)[:, None] == (chip * SLOTS + slot)[None, :])
    tags = jnp.max(jnp.where(placed, code[None, :], -1), axis=1).reshape(1, chips * SLOTS)
    tags = tags.astype(jnp.bfloat16)
    tags = lax.all_gather(tags, ("x", "z", "c"), axis=0, tiled=True)
    my_chip = lax.axis_index("x") * lax.axis_size("z") + lax.axis_index("z")
    tags = lax.dynamic_slice_in_dim(tags, my_chip * SLOTS, SLOTS, 1).astype(jnp.int32)
    my_core = lax.axis_index("c").reshape(1)
    outgoing = make_units(three_center, coefficients, ao_block, chip, slot, chips)
    outgoing = outgoing.reshape(chips * 8, SLOTS, orbitals, LANES)
    incoming = lax.all_to_all(outgoing, AXES, split_axis=0, concat_axis=0, tiled=True)
    incoming = incoming.reshape(chips * cores, 4, SLOTS, orbitals, LANES)
    partial = make_exchange(tags, my_core, incoming, double_metric(metric_inv))
    width = ROWB * BLK
    partial = partial.reshape(4, width // 4, width)
    partial = lax.all_to_all(partial, "y", split_axis=0, concat_axis=0, tiled=True)
    return jnp.sum(partial, axis=0).astype(jnp.bfloat16)


def solution(mesh):
    split = Mesh(mesh.devices.reshape(4, 8, 2, 4), AXES)
    pair = ("x", "z", "c")
    in_specs = (P(pair, "y", None), P(), P(), P(pair, None), P(pair), P(pair), P(pair))
    out_specs = P(AXES, None)
    return jax.shard_map(body, mesh=split, in_specs=in_specs, out_specs=out_specs, check_vma=False)
```

```python
import functools

import jax
import jax.numpy as jnp
from jax import lax
from jax.experimental import pallas as pl
from jax.experimental.pallas import tpu as pltpu
from jax.sharding import Mesh, PartitionSpec as P

BLK = 64
AUXB = 8
ROWB = 8
NAUX = 512
LANES = 128
SLOTS = 4
MAIN = 3
GROUP = 4
PART = 16
AXES = ("x", "z", "c", "y")


def units_kernel(ao_ref, chip_ref, slot_ref, three_ref, coef_ref, spread_ref, main_ref, extra_ref, rows_ref, made_ref, got, sent):
    count, _, depth_in = rows_ref.shape
    tiles = depth_in // LANES
    depth = tiles * 8
    orbitals = coef_ref.shape[0]
    lane = lax.broadcasted_iota(jnp.int32, (orbitals, 8, depth), 2)
    row = lax.broadcasted_iota(jnp.int32, (orbitals, 8, depth), 1)
    keep = (lane % 8) == row
    low = lax.broadcasted_iota(jnp.int32, (orbitals // 2, 8, LANES), 2) < BLK

    def fetch(step):
        units = pl.ds(step * GROUP, GROUP)
        return pltpu.make_async_copy(three_ref.at[units], rows_ref.at[units], got.at[step])

    def send(unit, act):
        chip, slot = chip_ref[unit], slot_ref[unit]

        @pl.when(slot < MAIN)
        def _():
            act(pltpu.make_async_copy(made_ref.at[unit], main_ref.at[chip, :, slot], sent.at[unit]))

        @pl.when(slot >= MAIN)
        def _():
            act(pltpu.make_async_copy(made_ref.at[unit], extra_ref.at[chip, :, 0], sent.at[unit]))

    for step in range(count // GROUP):
        fetch(step).start()

    def group(step, carry):
        fetch(step).wait()
        spreads, rights = [], []
        for k in range(GROUP):
            ao = ao_ref[step * GROUP + k]
            picked = coef_ref[:, pl.ds(pl.multiple_of(ao // 2 * LANES, LANES), LANES)]
            spreads.append(jnp.dot(picked, spread_ref[ao % 2], preferred_element_type=jnp.float32))
        for k in range(GROUP):
            rows = rows_ref[step * GROUP + k].astype(jnp.float32)
            stacked = [
                jnp.concatenate([rows[h * 8 : h * 8 + 8, j * LANES : (j + 1) * LANES] for j in range(tiles)], axis=0)
                for h in range(2)
            ]
            right = jnp.concatenate(stacked, axis=1).astype(jnp.bfloat16)
            parts = []
            for parity in range(2):
                wide = spreads[k][:, None, parity * depth : (parity + 1) * depth]
                wide = jnp.broadcast_to(wide, (orbitals, 8, depth))
                left = jnp.where(keep, wide, 0.0).reshape(orbitals * 8, depth).astype(jnp.bfloat16)
                made = jnp.dot(left, right, preferred_element_type=jnp.float32)
                parts.append(made.reshape(orbitals // 2, 2, 8, 2 * LANES))
            done = []
            for h in range(2):
                cut = slice(h * LANES, (h + 1) * LANES)
                stay = jnp.where(low, parts[0][:, 0, :, cut], parts[1][:, 1, :, cut])
                move = jnp.where(low, parts[0][:, 1, :, cut], parts[1][:, 0, :, cut])
                done.append(stay + pltpu.roll(move, BLK, 2))
            units = jnp.stack(done, axis=1).reshape(orbitals * 8, LANES).astype(jnp.bfloat16)
            made_ref[step * GROUP + k] = units.reshape(8, orbitals, LANES)
        for k in range(GROUP):
            send(step * GROUP + k, lambda copy: copy.start())
        return carry

    lax.fori_loop(0, count // GROUP, group, 0)
    for unit in range(count):
        send(unit, lambda copy: copy.wait())


def make_units(three_center, coefficients, ao_block, chip, slot, chips):
    count, rows, depth = three_center.shape
    orbitals = coefficients.shape[0]
    wide = BLK // 2 * 8
    held = jnp.arange(LANES)[None, :, None]
    column = jnp.arange(2 * wide)[None, None, :]
    half = jnp.arange(2)[:, None, None]
    spread = (held == half * BLK + 2 * (column % wide // 8) + column // wide).astype(jnp.bfloat16)
    scalars = pl.BlockSpec(memory_space=pltpu.SMEM)
    return pl.pallas_call(
        units_kernel,
        in_specs=[scalars] * 3
        + [pl.BlockSpec(memory_space=pltpu.HBM)]
        + [pl.BlockSpec(memory_space=pltpu.VMEM)] * 2,
        out_specs=[pl.BlockSpec(memory_space=pltpu.HBM)] * 2,
        out_shape=[
            jax.ShapeDtypeStruct((chips, 8, MAIN, orbitals, LANES), jnp.bfloat16),
            jax.ShapeDtypeStruct((chips, 8, SLOTS - MAIN, orbitals, LANES), jnp.bfloat16),
        ],
        scratch_shapes=[
            pltpu.VMEM((count, rows, depth), jnp.bfloat16),
            pltpu.VMEM((count, 8, orbitals, LANES), jnp.bfloat16),
            pltpu.SemaphoreType.DMA((count // GROUP,)),
            pltpu.SemaphoreType.DMA((count,)),
        ],
        compiler_params=pltpu.CompilerParams(vmem_limit_bytes=60 * 1024 * 1024),
        name="units",
    )(ao_block, chip, slot, three_center, coefficients, spread)


def own_exchange(whole, metric_ref, fitted, out_ref, first):
    fitted[...] = jnp.dot(whole, metric_ref[...], preferred_element_type=jnp.float32).astype(jnp.bfloat16)
    part = lax.dot_general(fitted[...], whole, (((1,), (1,)), ((), ())), preferred_element_type=jnp.float32)
    if first:
        out_ref[...] = part
    else:
        out_ref[...] += part


def gather_kernel(list_ref, filled_ref, core_ref, in_ref, metric_ref, mine_ref, out_ref, total, fitted):
    step = pl.program_id(0)
    quarters, slots = in_ref.shape[1], in_ref.shape[2]

    @pl.when(step == 0)
    def _():
        total[...] = jnp.zeros_like(total)

    def add(k, carry):
        entry = list_ref[step, k]
        spot, tag = entry // (2 * ROWB * AUXB), entry % (2 * ROWB * AUXB)
        source, slot = spot // slots, spot % slots
        owner, row, aux = tag // (ROWB * AUXB), tag // AUXB % ROWB, tag % AUXB
        places = [
            (owner, pair, aux, pl.ds(pl.multiple_of(row * BLK + quarter * 16, 16), 16), slice(None))
            for quarter in range(quarters)
            for pair in range(2)
        ]
        news = [
            in_ref[source, quarter, slot, pair * 16 : pair * 16 + 16, :].astype(jnp.float32)
            for quarter in range(quarters)
            for pair in range(2)
        ]
        sums = [total[place] + new for place, new in zip(places, news)]
        for place, value in zip(places, sums):
            total[place] = value
        return carry

    lax.fori_loop(0, filled_ref[step], add, 0)

    @pl.when(step == pl.num_programs(0) - 1)
    def _():
        mine = core_ref[0]
        for pair in range(2):
            whole = [total[1 - mine, pair, aux].astype(jnp.bfloat16) for aux in range(AUXB)]
            own_exchange(jnp.concatenate(whole, axis=1), metric_ref, fitted, out_ref, pair == 0)
        for pair in range(2):
            for aux in range(AUXB):
                mine_ref[pair, :, aux * LANES : (aux + 1) * LANES] = total[mine, pair, aux].astype(jnp.bfloat16)


def rest_kernel(mine_ref, metric_ref, out_ref, fitted):
    for pair in range(2):
        own_exchange(mine_ref[pair], metric_ref, fitted, out_ref, pair == 0)


def filled_list(tags):
    sources, slots = tags.shape
    tags = tags.reshape(sources // PART, PART * slots)
    filled = tags >= 0
    spot = jnp.arange(PART * slots, dtype=jnp.int32)
    before = spot[:, None] < spot[None, :]
    place = jnp.sum((filled[:, :, None] & before[None]).astype(jnp.int32), axis=1)
    here = filled[:, :, None] & (place[:, :, None] == spot)
    entry = spot * (2 * ROWB * AUXB) + tags
    return jnp.sum(jnp.where(here, entry[:, :, None], 0), axis=1), jnp.sum(filled.astype(jnp.int32), axis=1)


def gather_exchange(entries, filled, core, incoming, metric):
    sources, quarters, slots, rows, lanes = incoming.shape
    width = ROWB * BLK
    inner = AUXB * lanes
    grid_spec = pltpu.PrefetchScalarGridSpec(
        num_scalar_prefetch=3,
        grid=(sources // PART,),
        in_specs=[
            pl.BlockSpec((PART, quarters, slots, rows, lanes), lambda s, entries, filled, core: (s, 0, 0, 0, 0)),
            pl.BlockSpec(metric.shape, lambda s, entries, filled, core: (0, 0)),
        ],
        out_specs=[
            pl.BlockSpec((2, width, inner), lambda s, entries, filled, core: (0, 0, 0)),
            pl.BlockSpec((width, width), lambda s, entries, filled, core: (0, 0)),
        ],
        scratch_shapes=[
            pltpu.VMEM((2, 2, AUXB, width, lanes), jnp.float32),
            pltpu.VMEM((width, inner), jnp.bfloat16),
        ],
    )
    return pl.pallas_call(
        gather_kernel,
        grid_spec=grid_spec,
        out_shape=[
            jax.ShapeDtypeStruct((2, width, inner), jnp.bfloat16),
            jax.ShapeDtypeStruct((width, width), jnp.float32),
        ],
        compiler_params=pltpu.CompilerParams(vmem_limit_bytes=48 * 1024 * 1024),
        name="gather_exchange",
    )(entries, filled, core, incoming, metric)


def rest_exchange(mine, metric):
    _, width, inner = mine.shape
    flops = 4 * width * inner * (inner + width)
    return pl.pallas_call(
        rest_kernel,
        out_shape=jax.ShapeDtypeStruct((width, width), jnp.float32),
        scratch_shapes=[pltpu.VMEM((width, inner), jnp.bfloat16)],
        compiler_params=pltpu.CompilerParams(vmem_limit_bytes=48 * 1024 * 1024),
        cost_estimate=pl.CostEstimate(flops=flops, bytes_accessed=5 * width * inner * 2, transcendentals=0),
        name="own_exchange",
    )(mine, metric)


def double_metric(metric_inv):
    blocks = metric_inv.reshape(AUXB, 1, BLK, AUXB, 1, BLK)
    same = jnp.eye(2, dtype=jnp.bool_).reshape(1, 2, 1, 1, 2, 1)
    return jnp.where(same, blocks, 0).reshape(2 * NAUX, 2 * NAUX)


def body(three_center, coefficients, metric_inv, target_owner, row_slot, aux_block, ao_block):
    count, rows, depth = three_center.shape
    orbitals = coefficients.shape[0]
    cores = lax.axis_size("c")
    chips = lax.axis_size("x") * lax.axis_size("z")
    target = target_owner[:, 0]
    chip, core = target // cores, target % cores
    code = core * (ROWB * AUXB) + row_slot * AUXB + aux_block
    counter = jnp.arange(count, dtype=jnp.int32)
    earlier = (chip[:, None] == chip[None, :]) & (counter[None, :] < counter[:, None])
    slot = jnp.sum(earlier.astype(jnp.int32), axis=1)
    placed = (jnp.arange(chips * SLOTS, dtype=jnp.int32)[:, None] == (chip * SLOTS + slot)[None, :])
    tags = jnp.max(jnp.where(placed, code[None, :], -1), axis=1).reshape(chips, SLOTS)
    more = jnp.broadcast_to(jnp.max(tags[:, MAIN:]), (chips, 1))
    tags = jnp.concatenate([tags, more], axis=1)[:, None]
    tags = jnp.broadcast_to(tags, (chips, cores, SLOTS + 1)).reshape(chips * cores, SLOTS + 1)
    tags = lax.all_to_all(tags, ("x", "z", "c"), split_axis=0, concat_axis=0, tiled=True)
    my_core = lax.axis_index("c").reshape(1)
    main, extra = make_units(three_center, coefficients, ao_block, chip, slot, chips)
    main = main.reshape(chips * 8, MAIN, orbitals, LANES)
    extra = extra.reshape(chips * 8, SLOTS - MAIN, orbitals, LANES)
    main = lax.all_to_all(main, AXES, split_axis=0, concat_axis=0, tiled=True)
    metric = double_metric(metric_inv)

    few_list, many_list = lax.optimization_barrier((filled_list(tags[:, :MAIN]), filled_list(tags[:, :SLOTS])))

    def few(main, extra, few_list, many_list, core, metric):
        main = main.reshape(chips * cores, 4, MAIN, orbitals, LANES)
        return gather_exchange(*few_list, core, main, metric)

    def many(main, extra, few_list, many_list, core, metric):
        extra = lax.all_to_all(extra, AXES, split_axis=0, concat_axis=0, tiled=True)
        both = jnp.concatenate([main, extra], axis=1).reshape(chips * cores, 4, SLOTS, orbitals, LANES)
        return gather_exchange(*many_list, core, both, metric)

    overflow = jnp.max(tags[:, SLOTS]) >= 0
    mine, sent = lax.cond(overflow, many, few, main, extra, few_list, many_list, my_core, metric)
    got = lax.ppermute(sent, "c", [(0, 1), (1, 0)])
    partial = rest_exchange(mine, metric) + got
    width = ROWB * BLK
    partial = partial.reshape(4, width // 4, width)
    partial = lax.all_to_all(partial, "y", split_axis=0, concat_axis=0, tiled=True)
    return jnp.sum(partial, axis=0).astype(jnp.bfloat16)


def solution(mesh):
    split = Mesh(mesh.devices.reshape(4, 8, 2, 4), AXES)
    pair = ("x", "z", "c")
    in_specs = (P(pair, "y", None), P(), P(), P(pair, None), P(pair), P(pair), P(pair))
    out_specs = P(AXES, None)
    return jax.shard_map(body, mesh=split, in_specs=in_specs, out_specs=out_specs, check_vma=False)
```

```python
import functools

import jax
import jax.numpy as jnp
from jax import lax
from jax.experimental import pallas as pl
from jax.experimental.pallas import tpu as pltpu
from jax.sharding import Mesh, PartitionSpec as P

BLK = 64
AUXB = 8
ROWB = 8
NAUX = 512
LANES = 128
SLOTS = 4
MAIN = 3
GROUP = 4
PART = 16
AXES = ("x", "z", "c", "y")
AWAY = ("c", "x", "y", "z")


def units_kernel(
    owner_ref, row_ref, aux_ref, ao_ref, three_ref, coef_ref,
    main_ref, extra_ref, tag_ref, rows_ref, made_ref, spread_ref, chip_ref, slot_ref, got, sent
):
    count, _, depth_in = rows_ref.shape
    tiles = depth_in // LANES
    depth = tiles * 8
    orbitals = coef_ref.shape[0]
    chips, columns = tag_ref.shape
    depths = main_ref.shape[3]

    def fetch(step):
        units = pl.ds(step * GROUP, GROUP)
        return pltpu.make_async_copy(three_ref.at[units], rows_ref.at[units], got.at[step])

    def send(unit, act):
        chip, slot = chip_ref[unit], slot_ref[unit]
        across, along = chip // depths, chip % depths

        @pl.when(slot < MAIN)
        def _():
            act(pltpu.make_async_copy(made_ref.at[unit], main_ref.at[:, across, :, along, slot], sent.at[unit]))

        @pl.when(slot >= MAIN)
        def _():
            act(pltpu.make_async_copy(made_ref.at[unit], extra_ref.at[:, across, :, along, 0], sent.at[unit]))

    for step in range(count // GROUP):
        fetch(step).start()

    held = lax.broadcasted_iota(jnp.int32, (LANES, 2 * depth), 0)
    column = lax.broadcasted_iota(jnp.int32, (LANES, 2 * depth), 1)
    source = 2 * (column % depth // 8) + column // depth
    for half in range(2):
        spread_ref[half] = jnp.where(held == half * BLK + source, 1.0, 0.0).astype(jnp.bfloat16)

    def clear(chip, carry):
        for k in range(columns):
            tag_ref[chip, k] = -1 if k < SLOTS else 0
        return carry

    lax.fori_loop(0, chips, clear, 0)

    def rank(unit, fullest):
        owner = owner_ref[unit]
        chip = owner // 2
        slot = tag_ref[chip, SLOTS]
        chip_ref[unit] = chip
        slot_ref[unit] = slot
        tag_ref[chip, slot] = owner % 2 * (ROWB * AUXB) + row_ref[unit] * AUXB + aux_ref[unit]
        tag_ref[chip, SLOTS] = slot + 1
        return jnp.maximum(fullest, slot + 1)

    fullest = lax.fori_loop(0, count, rank, 0)

    def note(chip, carry):
        tag_ref[chip, SLOTS] = fullest
        return carry

    lax.fori_loop(0, chips, note, 0)

    lane = lax.broadcasted_iota(jnp.int32, (orbitals, 8, depth), 2)
    row = lax.broadcasted_iota(jnp.int32, (orbitals, 8, depth), 1)
    keep = (lane % 8) == row
    low = lax.broadcasted_iota(jnp.int32, (orbitals // 2, 8, LANES), 2) < BLK

    def group(step, carry):
        fetch(step).wait()
        spreads = []
        for k in range(GROUP):
            ao = ao_ref[step * GROUP + k]
            picked = coef_ref[:, pl.ds(pl.multiple_of(ao // 2 * LANES, LANES), LANES)]
            spreads.append(jnp.dot(picked, spread_ref[ao % 2], preferred_element_type=jnp.float32))
        for k in range(GROUP):
            rows = rows_ref[step * GROUP + k].astype(jnp.float32)
            stacked = [
                jnp.concatenate([rows[h * 8 : h * 8 + 8, j * LANES : (j + 1) * LANES] for j in range(tiles)], axis=0)
                for h in range(2)
            ]
            right = jnp.concatenate(stacked, axis=1).astype(jnp.bfloat16)
            parts = []
            for parity in range(2):
                wide = spreads[k][:, None, parity * depth : (parity + 1) * depth]
                wide = jnp.broadcast_to(wide, (orbitals, 8, depth))
                left = jnp.where(keep, wide, 0.0).reshape(orbitals * 8, depth).astype(jnp.bfloat16)
                made = jnp.dot(left, right, preferred_element_type=jnp.float32)
                parts.append(made.reshape(orbitals // 2, 2, 8, 2 * LANES))
            done = []
            for h in range(2):
                cut = slice(h * LANES, (h + 1) * LANES)
                stay = jnp.where(low, parts[0][:, 0, :, cut], parts[1][:, 1, :, cut])
                move = jnp.where(low, parts[0][:, 1, :, cut], parts[1][:, 0, :, cut])
                done.append(stay + pltpu.roll(move, BLK, 2))
            units = jnp.stack(done, axis=1).reshape(orbitals * 8, LANES).astype(jnp.bfloat16)
            made_ref[step * GROUP + k] = units.reshape(2, 4, orbitals, LANES)
        for k in range(GROUP):
            send(step * GROUP + k, lambda copy: copy.start())
        return carry

    lax.fori_loop(0, count // GROUP, group, 0)
    for unit in range(count):
        send(unit, lambda copy: copy.wait())


def make_units(three_center, coefficients, owner, row_slot, aux_block, ao_block, chips):
    count, rows, depth = three_center.shape
    orbitals = coefficients.shape[0]
    across, along = chips
    scalars = pl.BlockSpec(memory_space=pltpu.SMEM)
    main = (2, across, 4, along, MAIN, orbitals, LANES)
    extra = (2, across, 4, along, SLOTS - MAIN, orbitals, LANES)
    return pl.pallas_call(
        units_kernel,
        in_specs=[scalars] * 4
        + [pl.BlockSpec(memory_space=pltpu.HBM), pl.BlockSpec(memory_space=pltpu.VMEM)],
        out_specs=[pl.BlockSpec(memory_space=pltpu.HBM)] * 2 + [scalars],
        out_shape=[
            jax.ShapeDtypeStruct(main, jnp.bfloat16),
            jax.ShapeDtypeStruct(extra, jnp.bfloat16),
            jax.ShapeDtypeStruct((across * along, 8), jnp.int32),
        ],
        scratch_shapes=[
            pltpu.VMEM((count, rows, depth), jnp.bfloat16),
            pltpu.VMEM((count, 2, 4, orbitals, LANES), jnp.bfloat16),
            pltpu.VMEM((2, LANES, BLK * 8), jnp.bfloat16),
            pltpu.SMEM((count,), jnp.int32),
            pltpu.SMEM((count,), jnp.int32),
            pltpu.SemaphoreType.DMA((count // GROUP,)),
            pltpu.SemaphoreType.DMA((count,)),
        ],
        compiler_params=pltpu.CompilerParams(vmem_limit_bytes=60 * 1024 * 1024),
        name="units",
    )(owner, row_slot, aux_block, ao_block, three_center, coefficients)


def own_exchange(whole, metric_ref, fitted, out_ref, first):
    fitted[...] = jnp.dot(whole, metric_ref[...], preferred_element_type=jnp.float32).astype(jnp.bfloat16)
    part = lax.dot_general(fitted[...], whole, (((1,), (1,)), ((), ())), preferred_element_type=jnp.float32)
    if first:
        out_ref[...] = part
    else:
        out_ref[...] += part


def gather_kernel(tag_ref, place_ref, in_ref, metric_ref, mine_ref, out_ref, total, fitted):
    step = pl.program_id(0)
    planes, quarters, depths, slots = in_ref.shape[:4]
    columns = pl.num_programs(0) * planes // 2

    @pl.when(step == 0)
    def _():
        total[...] = jnp.zeros_like(total)

    def add(k, carry):
        source, slot = k // slots, k % slots
        plane, depth = source // depths, source % depths
        column, core = (step * planes + plane) % columns, (step * planes + plane) // columns
        away = (place_ref[2] - depth + depths - 1) % depths * columns + (place_ref[1] - column + columns) % columns
        tag = tag_ref[away * 2 + core, slot]

        @pl.when(tag >= 0)
        def _():
            owner, row, aux = tag // (ROWB * AUXB), tag // AUXB % ROWB, tag % AUXB
            spots = [
                (owner, pair, aux, pl.ds(pl.multiple_of(row * BLK + quarter * 16, 16), 16), slice(None))
                for quarter in range(quarters)
                for pair in range(2)
            ]
            news = [
                in_ref[plane, quarter, depth, slot, pair * 16 : pair * 16 + 16, :].astype(jnp.float32)
                for quarter in range(quarters)
                for pair in range(2)
            ]
            sums = [total[spot] + new for spot, new in zip(spots, news)]
            for spot, value in zip(spots, sums):
                total[spot] = value

        return carry

    lax.fori_loop(0, planes * depths * slots, add, 0)

    @pl.when(step == pl.num_programs(0) - 1)
    def _():
        mine = place_ref[0]
        for pair in range(2):
            whole = [total[1 - mine, pair, aux].astype(jnp.bfloat16) for aux in range(AUXB)]
            own_exchange(jnp.concatenate(whole, axis=1), metric_ref, fitted, out_ref, pair == 0)
        for pair in range(2):
            for aux in range(AUXB):
                mine_ref[pair, :, aux * LANES : (aux + 1) * LANES] = total[mine, pair, aux].astype(jnp.bfloat16)


def rest_kernel(mine_ref, metric_ref, out_ref, fitted):
    for pair in range(2):
        own_exchange(mine_ref[pair], metric_ref, fitted, out_ref, pair == 0)


def gather_exchange(tags, place, incoming, metric):
    planes, quarters, depths, slots, rows, lanes = incoming.shape
    each = PART // depths
    width = ROWB * BLK
    inner = AUXB * lanes
    grid_spec = pltpu.PrefetchScalarGridSpec(
        num_scalar_prefetch=2,
        grid=(planes // each,),
        in_specs=[
            pl.BlockSpec(
                (each, quarters, depths, slots, rows, lanes), lambda s, tags, place: (s, 0, 0, 0, 0, 0)
            ),
            pl.BlockSpec(metric.shape, lambda s, tags, place: (0, 0)),
        ],
        out_specs=[
            pl.BlockSpec((2, width, inner), lambda s, tags, place: (0, 0, 0)),
            pl.BlockSpec((width, width), lambda s, tags, place: (0, 0)),
        ],
        scratch_shapes=[
            pltpu.VMEM((2, 2, AUXB, width, lanes), jnp.float32),
            pltpu.VMEM((width, inner), jnp.bfloat16),
        ],
    )
    return pl.pallas_call(
        gather_kernel,
        grid_spec=grid_spec,
        out_shape=[
            jax.ShapeDtypeStruct((2, width, inner), jnp.bfloat16),
            jax.ShapeDtypeStruct((width, width), jnp.float32),
        ],
        compiler_params=pltpu.CompilerParams(vmem_limit_bytes=48 * 1024 * 1024),
        name="gather_exchange",
    )(tags, place, incoming, metric)


def rest_exchange(mine, metric):
    _, width, inner = mine.shape
    flops = 4 * width * inner * (inner + width)
    return pl.pallas_call(
        rest_kernel,
        out_shape=jax.ShapeDtypeStruct((width, width), jnp.float32),
        scratch_shapes=[pltpu.VMEM((width, inner), jnp.bfloat16)],
        compiler_params=pltpu.CompilerParams(vmem_limit_bytes=48 * 1024 * 1024),
        cost_estimate=pl.CostEstimate(flops=flops, bytes_accessed=5 * width * inner * 2, transcendentals=0),
        name="own_exchange",
    )(mine, metric)


def double_metric(metric_inv):
    blocks = metric_inv.reshape(AUXB, 1, BLK, AUXB, 1, BLK)
    same = jnp.eye(2, dtype=jnp.bool_).reshape(1, 2, 1, 1, 2, 1)
    return jnp.where(same, blocks, 0).reshape(2 * NAUX, 2 * NAUX)


def part(table, index, axis):
    return lax.dynamic_index_in_dim(table, index, axis, keepdims=False)


def share_tags(tags, across, along):
    core, column, depth = lax.axis_index("c"), lax.axis_index("x"), lax.axis_index("z")
    swap = [(0, 1), (1, 0)]
    first = core == 0
    other = lax.ppermute(tags, "c", swap)
    both = jnp.where(first, jnp.stack([tags, other]), jnp.stack([other, tags])).reshape(2, across, along, 8)
    rows = [part(both, column, 1)]
    for away in range(1, across):
        steps = [(k, (k + away) % across) for k in range(across)]
        rows.append(lax.ppermute(part(both, (column + away) % across, 1), "x", steps))
    table = jnp.stack(rows)
    half = along // 2
    rows = []
    for away in range(1, half + 1):
        steps = [(z * 2 + c, (z + away + half * c) % along * 2 + c) for z in range(along) for c in range(2)]
        rows.append(lax.ppermute(part(table, (depth + away + half * core) % along, 2), ("z", "c"), steps))
    rows = jnp.stack(rows)
    other = lax.ppermute(rows, "c", swap)
    return jnp.where(first, jnp.concatenate([rows, other]), jnp.concatenate([other, rows]))


def body(three_center, coefficients, metric_inv, target_owner, row_slot, aux_block, ao_block):
    orbitals = coefficients.shape[0]
    cores, across, along = lax.axis_size("c"), lax.axis_size("x"), lax.axis_size("z")
    main, extra, tags = make_units(
        three_center, coefficients, target_owner[:, 0], row_slot, aux_block, ao_block, (across, along)
    )
    devices = cores * across * 4 * along
    main = main.reshape(devices, MAIN, orbitals, LANES)
    extra = extra.reshape(devices, SLOTS - MAIN, orbitals, LANES)
    main = lax.all_to_all(main, AWAY, split_axis=0, concat_axis=0, tiled=True)
    metric = double_metric(metric_inv)

    tags = share_tags(tags, across, along).reshape(cores * across * along, 8)
    place = jnp.stack([lax.axis_index("c"), lax.axis_index("x"), lax.axis_index("z")])

    def finish(tags, incoming, place, metric):
        incoming = incoming.reshape(cores * across, 4, along, -1, orbitals, LANES)
        mine, sent = gather_exchange(tags, place, incoming, metric)
        got = lax.ppermute(sent, "c", [(0, 1), (1, 0)])
        return rest_exchange(mine, metric) + got

    def few(main, extra, tags, place, metric):
        return finish(tags, main, place, metric)

    def many(main, extra, tags, place, metric):
        extra = lax.all_to_all(extra, AWAY, split_axis=0, concat_axis=0, tiled=True)
        return finish(tags, jnp.concatenate([main, extra], axis=1), place, metric)

    overflow = jnp.max(tags[:, SLOTS]) > MAIN
    partial = lax.cond(overflow, many, few, main, extra, tags, place, metric)
    width = ROWB * BLK
    partial = partial.reshape(4, width // 4, width)
    partial = lax.all_to_all(partial, "y", split_axis=0, concat_axis=0, tiled=True)
    return jnp.sum(partial, axis=0).astype(jnp.bfloat16)


def solution(mesh):
    split = Mesh(mesh.devices.reshape(4, 8, 2, 4), AXES)
    pair = ("x", "z", "c")
    in_specs = (P(pair, "y", None), P(), P(), P(pair, None), P(pair), P(pair), P(pair))
    out_specs = P(AXES, None)
    return jax.shard_map(body, mesh=split, in_specs=in_specs, out_specs=out_specs, check_vma=False)
```

```python
import functools

import jax
import jax.numpy as jnp
from jax import lax
from jax.experimental import pallas as pl
from jax.experimental.pallas import tpu as pltpu
from jax.sharding import Mesh, PartitionSpec as P

BLK = 64
AUXB = 8
ROWB = 8
NAUX = 512
LANES = 128
SLOTS = 4
MAIN = 3
GROUP = 12
PARTS = 4
FETCH = 4
AXES = ("x", "z", "c", "y")
AWAY = ("c", "x", "y", "z")


def units_kernel(
    owner_ref, row_ref, aux_ref, ao_ref, three_ref, coef_ref,
    main_ref, extra_ref, tag_ref, rows_ref, made_ref, held_ref, spread_ref, chip_ref, slot_ref, got, sent
):
    count, _, depth_in = rows_ref.shape
    tiles = depth_in // LANES
    depth = tiles * 8
    orbitals = coef_ref.shape[0]
    chips, columns = tag_ref.shape
    depths = main_ref.shape[3]

    def fetch(step):
        units = pl.ds(step * FETCH, FETCH)
        return pltpu.make_async_copy(three_ref.at[units], rows_ref.at[units], got.at[step])

    orbitals_held = pltpu.make_async_copy(coef_ref, held_ref, got.at[count // FETCH])
    orbitals_held.start()

    def send(unit, act):
        chip, slot = chip_ref[unit], slot_ref[unit]
        across, along = chip // depths, chip % depths

        @pl.when(slot < MAIN)
        def _():
            act(pltpu.make_async_copy(made_ref.at[unit], main_ref.at[:, across, :, along, slot], sent.at[unit]))

        @pl.when(slot >= MAIN)
        def _():
            act(pltpu.make_async_copy(made_ref.at[unit], extra_ref.at[:, across, :, along, 0], sent.at[unit]))

    for step in range(count // FETCH):
        fetch(step).start()

    held = lax.broadcasted_iota(jnp.int32, (LANES, 2 * depth), 0)
    column = lax.broadcasted_iota(jnp.int32, (LANES, 2 * depth), 1)
    source = 2 * (column % depth // 8) + column // depth
    for half in range(2):
        spread_ref[half] = jnp.where(held == half * BLK + source, 1.0, 0.0).astype(jnp.bfloat16)

    def clear(chip, carry):
        for k in range(columns):
            tag_ref[chip, k] = -1 if k < SLOTS else 0
        return carry

    lax.fori_loop(0, chips, clear, 0)

    def rank(unit, fullest):
        owner = owner_ref[unit]
        chip = owner // 2
        slot = tag_ref[chip, SLOTS]
        chip_ref[unit] = chip
        slot_ref[unit] = slot
        tag_ref[chip, slot] = owner % 2 * (ROWB * AUXB) + row_ref[unit] * AUXB + aux_ref[unit]
        tag_ref[chip, SLOTS] = slot + 1
        return jnp.maximum(fullest, slot + 1)

    fullest = lax.fori_loop(0, count, rank, 0)

    def note(chip, carry):
        tag_ref[chip, SLOTS] = fullest
        return carry

    lax.fori_loop(0, chips, note, 0)

    lane = lax.broadcasted_iota(jnp.int32, (orbitals, 8, depth), 2)
    row = lax.broadcasted_iota(jnp.int32, (orbitals, 8, depth), 1)
    keep = (lane & 7) == row
    low = lax.broadcasted_iota(jnp.int32, (orbitals // 2, 8, LANES), 2) < BLK

    orbitals_held.wait()

    def group(step, carry):
        for k in range(GROUP // FETCH):
            fetch(step * (GROUP // FETCH) + k).wait()
        spreads = []
        for k in range(GROUP):
            ao = ao_ref[step * GROUP + k]
            picked = held_ref[:, pl.ds(pl.multiple_of(ao // 2 * LANES, LANES), LANES)]
            spreads.append(jnp.dot(picked, spread_ref[ao % 2], preferred_element_type=jnp.float32))
        for k in range(GROUP):
            rows = rows_ref[step * GROUP + k].astype(jnp.float32)
            stacked = [
                jnp.concatenate([rows[h * 8 : h * 8 + 8, j * LANES : (j + 1) * LANES] for j in range(tiles)], axis=0)
                for h in range(2)
            ]
            right = jnp.concatenate(stacked, axis=1).astype(jnp.bfloat16)
            parts = []
            for parity in range(2):
                wide = spreads[k][:, None, parity * depth : (parity + 1) * depth]
                wide = jnp.broadcast_to(wide, (orbitals, 8, depth))
                left = jnp.where(keep, wide, 0.0).reshape(orbitals * 8, depth).astype(jnp.bfloat16)
                made = jnp.dot(left, right, preferred_element_type=jnp.float32)
                parts.append(made.reshape(orbitals // 2, 2, 8, 2 * LANES))
            done = []
            for h in range(2):
                cut = slice(h * LANES, (h + 1) * LANES)
                stay = jnp.where(low, parts[0][:, 0, :, cut], parts[1][:, 1, :, cut])
                move = jnp.where(low, parts[0][:, 1, :, cut], parts[1][:, 0, :, cut])
                done.append(stay + pltpu.roll(move, BLK, 2))
            units = jnp.stack(done, axis=1).reshape(orbitals * 8, LANES).astype(jnp.bfloat16)
            made_ref[step * GROUP + k] = units.reshape(2, 4, orbitals, LANES)
        for k in range(GROUP):
            send(step * GROUP + k, lambda copy: copy.start())
        return carry

    lax.fori_loop(0, count // GROUP, group, 0)
    for unit in range(count):
        send(unit, lambda copy: copy.wait())


def make_units(three_center, coefficients, owner, row_slot, aux_block, ao_block, chips):
    count, rows, depth = three_center.shape
    orbitals = coefficients.shape[0]
    across, along = chips
    scalars = pl.BlockSpec(memory_space=pltpu.SMEM)
    main = (2, across, 4, along, MAIN, orbitals, LANES)
    extra = (2, across, 4, along, SLOTS - MAIN, orbitals, LANES)
    return pl.pallas_call(
        units_kernel,
        in_specs=[scalars] * 4
        + [pl.BlockSpec(memory_space=pltpu.HBM)] * 2,
        out_specs=[pl.BlockSpec(memory_space=pltpu.HBM)] * 2 + [scalars],
        out_shape=[
            jax.ShapeDtypeStruct(main, jnp.bfloat16),
            jax.ShapeDtypeStruct(extra, jnp.bfloat16),
            jax.ShapeDtypeStruct((across * along, 8), jnp.int32),
        ],
        scratch_shapes=[
            pltpu.VMEM((count, rows, depth), jnp.bfloat16),
            pltpu.VMEM((count, 2, 4, orbitals, LANES), jnp.bfloat16),
            pltpu.VMEM(coefficients.shape, jnp.bfloat16),
            pltpu.VMEM((2, LANES, BLK * 8), jnp.bfloat16),
            pltpu.SMEM((count,), jnp.int32),
            pltpu.SMEM((count,), jnp.int32),
            pltpu.SemaphoreType.DMA((count // FETCH + 1,)),
            pltpu.SemaphoreType.DMA((count,)),
        ],
        compiler_params=pltpu.CompilerParams(vmem_limit_bytes=60 * 1024 * 1024),
        name="units",
    )(owner, row_slot, aux_block, ao_block, three_center, coefficients)


def own_exchange(whole, metric_ref, fitted, out_ref, first):
    fitted[...] = jnp.dot(whole, metric_ref[...], preferred_element_type=jnp.float32).astype(jnp.bfloat16)
    part = lax.dot_general(fitted[...], whole, (((1,), (1,)), ((), ())), preferred_element_type=jnp.float32)
    if first:
        out_ref[...] = part
    else:
        out_ref[...] += part


def gather_kernel(tag_ref, place_ref, in_ref, metric_ref, mine_ref, out_ref, total, fitted, held, got):
    groups, quarters, depths, slots = in_ref.shape[:4]
    columns = groups // 2
    planes = groups // PARTS

    def fetch(step):
        part = pl.ds(step * planes, planes)
        return pltpu.make_async_copy(in_ref.at[part], held.at[part], got.at[step])

    for step in range(PARTS):
        fetch(step).start()
    total[...] = jnp.zeros_like(total)

    def add(source, carry):
        group, depth = lax.shift_right_logical(source, 3), source & (depths - 1)
        core, column = lax.shift_right_logical(group, 2), group & (columns - 1)
        away = ((place_ref[2] - depth - 1) & (depths - 1)) * columns + ((place_ref[1] - column) & (columns - 1))
        for slot in range(slots):
            tag = tag_ref[away * 2 + core, slot]

            @pl.when(tag >= 0)
            def _():
                owner, row = lax.shift_right_logical(tag, 6), lax.shift_right_logical(tag, 3) & (ROWB - 1)
                aux = tag & (AUXB - 1)
                spots = [
                    (owner, pair, aux, pl.ds(pl.multiple_of(row * BLK + quarter * 16, 16), 16), slice(None))
                    for quarter in range(quarters)
                    for pair in range(2)
                ]
                news = [
                    held[group, quarter, depth, slot, pair * 16 : pair * 16 + 16, :].astype(jnp.float32)
                    for quarter in range(quarters)
                    for pair in range(2)
                ]
                sums = [total[spot] + new for spot, new in zip(spots, news)]
                for spot, value in zip(spots, sums):
                    total[spot] = value

        return carry

    for step in range(PARTS):
        fetch(step).wait()
        lax.fori_loop(step * planes * depths, (step + 1) * planes * depths, add, 0)

    mine = place_ref[0]
    for pair in range(2):
        whole = [total[1 - mine, pair, aux].astype(jnp.bfloat16) for aux in range(AUXB)]
        own_exchange(jnp.concatenate(whole, axis=1), metric_ref, fitted, out_ref, pair == 0)
    for pair in range(2):
        for aux in range(AUXB):
            mine_ref[pair, :, aux * LANES : (aux + 1) * LANES] = total[mine, pair, aux].astype(jnp.bfloat16)


def rest_kernel(mine_ref, metric_ref, out_ref, fitted):
    for pair in range(2):
        own_exchange(mine_ref[pair], metric_ref, fitted, out_ref, pair == 0)


def gather_exchange(tags, place, incoming, metric):
    lanes = incoming.shape[-1]
    width = ROWB * BLK
    inner = AUXB * lanes
    scalars = pl.BlockSpec(memory_space=pltpu.SMEM)
    held = pl.BlockSpec(memory_space=pltpu.VMEM)
    return pl.pallas_call(
        gather_kernel,
        in_specs=[scalars, scalars, pl.BlockSpec(memory_space=pltpu.HBM), held],
        out_specs=[held, held],
        out_shape=[
            jax.ShapeDtypeStruct((2, width, inner), jnp.bfloat16),
            jax.ShapeDtypeStruct((width, width), jnp.float32),
        ],
        scratch_shapes=[
            pltpu.VMEM((2, 2, AUXB, width, lanes), jnp.float32),
            pltpu.VMEM((width, inner), jnp.bfloat16),
            pltpu.VMEM(incoming.shape, incoming.dtype),
            pltpu.SemaphoreType.DMA((PARTS,)),
        ],
        compiler_params=pltpu.CompilerParams(vmem_limit_bytes=40 * 1024 * 1024),
        name="gather_exchange",
    )(tags, place, incoming, metric)


def rest_exchange(mine, metric):
    _, width, inner = mine.shape
    flops = 4 * width * inner * (inner + width)
    return pl.pallas_call(
        rest_kernel,
        out_shape=jax.ShapeDtypeStruct((width, width), jnp.float32),
        scratch_shapes=[pltpu.VMEM((width, inner), jnp.bfloat16)],
        compiler_params=pltpu.CompilerParams(vmem_limit_bytes=48 * 1024 * 1024),
        cost_estimate=pl.CostEstimate(flops=flops, bytes_accessed=5 * width * inner * 2, transcendentals=0),
        name="own_exchange",
    )(mine, metric)


def double_metric(metric_inv):
    blocks = metric_inv.reshape(AUXB, 1, BLK, AUXB, 1, BLK)
    same = jnp.eye(2, dtype=jnp.bool_).reshape(1, 2, 1, 1, 2, 1)
    return jnp.where(same, blocks, 0).reshape(2 * NAUX, 2 * NAUX)


def part(table, index, axis):
    return lax.dynamic_index_in_dim(table, index, axis, keepdims=False)


def share_tags(tags, across, along):
    core, column, depth = lax.axis_index("c"), lax.axis_index("x"), lax.axis_index("z")
    swap = [(0, 1), (1, 0)]
    first = core == 0
    other = lax.ppermute(tags, "c", swap)
    both = jnp.where(first, jnp.stack([tags, other]), jnp.stack([other, tags])).reshape(2, across, along, 8)
    rows = [part(both, column, 1)]
    for away in range(1, across):
        steps = [(k, (k + away) % across) for k in range(across)]
        rows.append(lax.ppermute(part(both, (column + away) % across, 1), "x", steps))
    table = jnp.stack(rows)
    half = along // 2
    rows = []
    for away in range(1, half + 1):
        steps = [(z * 2 + c, (z + away + half * c) % along * 2 + c) for z in range(along) for c in range(2)]
        rows.append(lax.ppermute(part(table, (depth + away + half * core) % along, 2), ("z", "c"), steps))
    rows = jnp.stack(rows)
    other = lax.ppermute(rows, "c", swap)
    return jnp.where(first, jnp.concatenate([rows, other]), jnp.concatenate([other, rows]))


def body(three_center, coefficients, metric_inv, target_owner, row_slot, aux_block, ao_block):
    orbitals = coefficients.shape[0]
    cores, across, along = lax.axis_size("c"), lax.axis_size("x"), lax.axis_size("z")
    main, extra, tags = make_units(
        three_center, coefficients, target_owner[:, 0], row_slot, aux_block, ao_block, (across, along)
    )
    devices = cores * across * 4 * along
    main = main.reshape(devices, MAIN, orbitals, LANES)
    extra = extra.reshape(devices, SLOTS - MAIN, orbitals, LANES)
    main = lax.all_to_all(main, AWAY, split_axis=0, concat_axis=0, tiled=True)
    metric = double_metric(metric_inv)

    tags = share_tags(tags, across, along).reshape(cores * across * along, 8)
    place = jnp.stack([lax.axis_index("c"), lax.axis_index("x"), lax.axis_index("z")])

    def finish(tags, incoming, place, metric):
        incoming = incoming.reshape(cores * across, 4, along, -1, orbitals, LANES)
        mine, sent = gather_exchange(tags, place, incoming, metric)
        got = lax.ppermute(sent, "c", [(0, 1), (1, 0)])
        return rest_exchange(mine, metric) + got

    def few(main, extra, tags, place, metric):
        return finish(tags, main, place, metric)

    def many(main, extra, tags, place, metric):
        extra = lax.all_to_all(extra, AWAY, split_axis=0, concat_axis=0, tiled=True)
        return finish(tags, jnp.concatenate([main, extra], axis=1), place, metric)

    overflow = jnp.max(tags[:, SLOTS]) > MAIN
    partial = lax.cond(overflow, many, few, main, extra, tags, place, metric)
    width = ROWB * BLK
    partial = partial.reshape(4, width // 4, width)
    partial = lax.all_to_all(partial, "y", split_axis=0, concat_axis=0, tiled=True)
    return jnp.sum(partial, axis=0).astype(jnp.bfloat16)


def solution(mesh):
    split = Mesh(mesh.devices.reshape(4, 8, 2, 4), AXES)
    pair = ("x", "z", "c")
    in_specs = (P(pair, "y", None), P(), P(), P(pair, None), P(pair), P(pair), P(pair))
    out_specs = P(AXES, None)
    return jax.shard_map(body, mesh=split, in_specs=in_specs, out_specs=out_specs, check_vma=False)
```

```python
import functools

import jax
import jax.numpy as jnp
from jax import lax
from jax.experimental import pallas as pl
from jax.experimental.pallas import tpu as pltpu
from jax.sharding import Mesh, PartitionSpec as P

BLK = 64
AUXB = 8
ROWB = 8
NAUX = 512
LANES = 128
SLOTS = 4
MAIN = 3
GROUP = 12
PARTS = 4
FETCH = 4
AXES = ("x", "z", "c", "y")
AWAY = ("c", "x", "y", "z")


def units_kernel(
    owner_ref, row_ref, aux_ref, ao_ref, three_ref, coef_ref,
    main_ref, extra_ref, tag_ref, rows_ref, made_ref, held_ref, spread_ref, chip_ref, slot_ref, got, sent
):
    count, _, depth_in = rows_ref.shape
    tiles = depth_in // LANES
    depth = tiles * 8
    orbitals = coef_ref.shape[0]
    chips, columns = tag_ref.shape
    depths = main_ref.shape[3]

    def fetch(step):
        units = pl.ds(step * FETCH, FETCH)
        return pltpu.make_async_copy(three_ref.at[units], rows_ref.at[units], got.at[step])

    orbitals_held = pltpu.make_async_copy(coef_ref, held_ref, got.at[count // FETCH])
    orbitals_held.start()

    def send(unit, act):
        chip, slot = chip_ref[unit], slot_ref[unit]
        across, along = chip // depths, chip % depths

        @pl.when(slot < MAIN)
        def _():
            act(pltpu.make_async_copy(made_ref.at[unit], main_ref.at[:, across, :, along, slot], sent.at[unit]))

        @pl.when(slot >= MAIN)
        def _():
            act(pltpu.make_async_copy(made_ref.at[unit], extra_ref.at[:, across, :, along, 0], sent.at[unit]))

    for step in range(count // FETCH):
        fetch(step).start()

    held = lax.broadcasted_iota(jnp.int32, (LANES, 2 * depth), 0)
    column = lax.broadcasted_iota(jnp.int32, (LANES, 2 * depth), 1)
    source = 2 * (column % depth // 8) + column // depth
    for half in range(2):
        spread_ref[half] = jnp.where(held == half * BLK + source, 1.0, 0.0).astype(jnp.bfloat16)

    def clear(chip, carry):
        for k in range(columns):
            tag_ref[chip, k] = -1 if k < SLOTS else 0
        return carry

    lax.fori_loop(0, chips, clear, 0)

    def rank(unit, fullest):
        owner = owner_ref[unit]
        chip = owner // 2
        slot = tag_ref[chip, SLOTS]
        chip_ref[unit] = chip
        slot_ref[unit] = slot
        tag_ref[chip, slot] = owner % 2 * (ROWB * AUXB) + row_ref[unit] * AUXB + aux_ref[unit]
        tag_ref[chip, SLOTS] = slot + 1
        return jnp.maximum(fullest, slot + 1)

    fullest = lax.fori_loop(0, count, rank, 0)

    def note(chip, carry):
        tag_ref[chip, SLOTS] = fullest
        return carry

    lax.fori_loop(0, chips, note, 0)

    lane = lax.broadcasted_iota(jnp.int32, (orbitals, 8, depth), 2)
    row = lax.broadcasted_iota(jnp.int32, (orbitals, 8, depth), 1)
    keep = (lane & 7) == row
    low = lax.broadcasted_iota(jnp.int32, (orbitals // 2, 8, LANES), 2) < BLK

    orbitals_held.wait()

    def group(step, carry):
        for k in range(GROUP // FETCH):
            fetch(step * (GROUP // FETCH) + k).wait()
        spreads = []
        for k in range(GROUP):
            ao = ao_ref[step * GROUP + k]
            picked = held_ref[:, pl.ds(pl.multiple_of(ao // 2 * LANES, LANES), LANES)]
            spreads.append(jnp.dot(picked, spread_ref[ao % 2], preferred_element_type=jnp.float32))
        for k in range(GROUP):
            rows = rows_ref[step * GROUP + k].astype(jnp.float32)
            stacked = [
                jnp.concatenate([rows[h * 8 : h * 8 + 8, j * LANES : (j + 1) * LANES] for j in range(tiles)], axis=0)
                for h in range(2)
            ]
            right = jnp.concatenate(stacked, axis=1).astype(jnp.bfloat16)
            parts = []
            for parity in range(2):
                wide = spreads[k][:, None, parity * depth : (parity + 1) * depth]
                wide = jnp.broadcast_to(wide, (orbitals, 8, depth))
                left = jnp.where(keep, wide, 0.0).reshape(orbitals * 8, depth).astype(jnp.bfloat16)
                made = jnp.dot(left, right, preferred_element_type=jnp.float32)
                parts.append(made.reshape(orbitals // 2, 2, 8, 2 * LANES))
            done = []
            for h in range(2):
                cut = slice(h * LANES, (h + 1) * LANES)
                stay = jnp.where(low, parts[0][:, 0, :, cut], parts[1][:, 1, :, cut])
                move = jnp.where(low, parts[0][:, 1, :, cut], parts[1][:, 0, :, cut])
                done.append(stay + pltpu.roll(move, BLK, 2))
            units = jnp.stack(done, axis=1).reshape(orbitals * 8, LANES).astype(jnp.bfloat16)
            made_ref[step * GROUP + k] = units.reshape(2, 4, orbitals, LANES)
        for k in range(GROUP):
            send(step * GROUP + k, lambda copy: copy.start())
        return carry

    lax.fori_loop(0, count // GROUP, group, 0)
    for unit in range(count):
        send(unit, lambda copy: copy.wait())


def make_units(three_center, coefficients, owner, row_slot, aux_block, ao_block, chips):
    count, rows, depth = three_center.shape
    orbitals = coefficients.shape[0]
    across, along = chips
    scalars = pl.BlockSpec(memory_space=pltpu.SMEM)
    main = (2, across, 4, along, MAIN, orbitals, LANES)
    extra = (2, across, 4, along, SLOTS - MAIN, orbitals, LANES)
    return pl.pallas_call(
        units_kernel,
        in_specs=[scalars] * 4
        + [pl.BlockSpec(memory_space=pltpu.HBM)] * 2,
        out_specs=[pl.BlockSpec(memory_space=pltpu.HBM)] * 2 + [scalars],
        out_shape=[
            jax.ShapeDtypeStruct(main, jnp.bfloat16),
            jax.ShapeDtypeStruct(extra, jnp.bfloat16),
            jax.ShapeDtypeStruct((across * along, 8), jnp.int32),
        ],
        scratch_shapes=[
            pltpu.VMEM((count, rows, depth), jnp.bfloat16),
            pltpu.VMEM((count, 2, 4, orbitals, LANES), jnp.bfloat16),
            pltpu.VMEM(coefficients.shape, jnp.bfloat16),
            pltpu.VMEM((2, LANES, BLK * 8), jnp.bfloat16),
            pltpu.SMEM((count,), jnp.int32),
            pltpu.SMEM((count,), jnp.int32),
            pltpu.SemaphoreType.DMA((count // FETCH + 1,)),
            pltpu.SemaphoreType.DMA((count,)),
        ],
        compiler_params=pltpu.CompilerParams(vmem_limit_bytes=60 * 1024 * 1024),
        name="units",
    )(owner, row_slot, aux_block, ao_block, three_center, coefficients)


def own_exchange(whole, metric_ref, fitted, out_ref, first):
    fitted[...] = jnp.dot(whole, metric_ref[...], preferred_element_type=jnp.float32).astype(jnp.bfloat16)
    part = lax.dot_general(fitted[...], whole, (((1,), (1,)), ((), ())), preferred_element_type=jnp.float32)
    if first:
        out_ref[...] = part
    else:
        out_ref[...] += part


def gather_kernel(tag_ref, place_ref, metric_ref, *refs):
    inputs = refs[: len(refs) - 6]
    mine_ref, out_ref, total, fitted, held, got = refs[len(refs) - 6 :]
    groups, quarters, depths, slots = held.shape[:4]
    columns = groups // 2
    planes = groups // PARTS

    def fetch(step):
        part = pl.ds(step * planes, planes)
        copies, first = [], 0
        for index, ref in enumerate(inputs):
            spots = pl.ds(first, ref.shape[3])
            copies.append(pltpu.make_async_copy(ref.at[part], held.at[part, :, :, spots], got.at[index, step]))
            first += ref.shape[3]
        return copies

    for step in range(PARTS):
        for copy in fetch(step):
            copy.start()
    total[...] = jnp.zeros_like(total)

    def add(source, carry):
        group, depth = lax.shift_right_logical(source, 3), source & (depths - 1)
        core, column = lax.shift_right_logical(group, 2), group & (columns - 1)
        away = (place_ref[2] - depth - 1) & (depths - 1)
        away = away ^ (place_ref[0] * (depths // 2))
        away = away * columns + ((place_ref[1] - column) & (columns - 1))
        for slot in range(slots):
            tag = tag_ref[away * 2 + core, slot]

            @pl.when(tag >= 0)
            def _():
                owner, row = lax.shift_right_logical(tag, 6), lax.shift_right_logical(tag, 3) & (ROWB - 1)
                aux = tag & (AUXB - 1)
                spots = [
                    (owner, pair, aux, pl.ds(pl.multiple_of(row * BLK + quarter * 16, 16), 16), slice(None))
                    for quarter in range(quarters)
                    for pair in range(2)
                ]
                news = [
                    held[group, quarter, depth, slot, pair * 16 : pair * 16 + 16, :].astype(jnp.float32)
                    for quarter in range(quarters)
                    for pair in range(2)
                ]
                sums = [total[spot] + new for spot, new in zip(spots, news)]
                for spot, value in zip(spots, sums):
                    total[spot] = value

        return carry

    for step in range(PARTS):
        for copy in fetch(step):
            copy.wait()
        lax.fori_loop(step * planes * depths, (step + 1) * planes * depths, add, 0)

    mine = place_ref[0]
    for pair in range(2):
        whole = [total[1 - mine, pair, aux].astype(jnp.bfloat16) for aux in range(AUXB)]
        own_exchange(jnp.concatenate(whole, axis=1), metric_ref, fitted, out_ref, pair == 0)
    for pair in range(2):
        for aux in range(AUXB):
            mine_ref[pair, :, aux * LANES : (aux + 1) * LANES] = total[mine, pair, aux].astype(jnp.bfloat16)


def rest_kernel(place_ref, mine_ref, metric_ref, before_ref, got_ref, *refs):
    outs, fitted = refs[:-1], refs[-1]
    whole = mine_ref[1]
    fitted[...] = jnp.dot(whole, metric_ref[...], preferred_element_type=jnp.float32).astype(jnp.bfloat16)
    share = outs[0].shape[0]
    for away, out_ref in enumerate(outs):
        rows = pl.ds(pl.multiple_of(((place_ref[3] + away) & (len(outs) - 1)) * share, share), share)
        made = lax.dot_general(fitted[rows], whole, (((1,), (1,)), ((), ())), preferred_element_type=jnp.float32)
        out_ref[...] = made + before_ref[rows] + got_ref[rows]


def half_kernel(mine_ref, metric_ref, out_ref, fitted):
    own_exchange(mine_ref[0], metric_ref, fitted, out_ref, True)


def gather_exchange(tags, place, incoming, metric):
    groups, quarters, depths, _, rows, lanes = incoming[0].shape
    slots = sum(array.shape[3] for array in incoming)
    width = ROWB * BLK
    inner = AUXB * lanes
    scalars = pl.BlockSpec(memory_space=pltpu.SMEM)
    held = pl.BlockSpec(memory_space=pltpu.VMEM)
    return pl.pallas_call(
        gather_kernel,
        in_specs=[scalars, scalars, held] + [pl.BlockSpec(memory_space=pltpu.HBM)] * len(incoming),
        out_specs=[held, held],
        out_shape=[
            jax.ShapeDtypeStruct((2, width, inner), jnp.bfloat16),
            jax.ShapeDtypeStruct((width, width), jnp.float32),
        ],
        scratch_shapes=[
            pltpu.VMEM((2, 2, AUXB, width, lanes), jnp.float32),
            pltpu.VMEM((width, inner), jnp.bfloat16),
            pltpu.VMEM((groups, quarters, depths, slots, rows, lanes), jnp.bfloat16),
            pltpu.SemaphoreType.DMA((len(incoming), PARTS)),
        ],
        compiler_params=pltpu.CompilerParams(vmem_limit_bytes=40 * 1024 * 1024),
        name="gather_exchange",
    )(tags, place, metric, *incoming)


def half_exchange(mine, metric):
    _, width, inner = mine.shape
    return pl.pallas_call(
        half_kernel,
        out_shape=jax.ShapeDtypeStruct((width, width), jnp.float32),
        scratch_shapes=[pltpu.VMEM((width, inner), jnp.bfloat16)],
        compiler_params=pltpu.CompilerParams(vmem_limit_bytes=40 * 1024 * 1024),
        cost_estimate=pl.CostEstimate(
            flops=2 * width * inner * (inner + width), bytes_accessed=5 * width * inner * 2, transcendentals=0
        ),
        name="half_exchange",
    )(mine, metric)


def rest_exchange(place, mine, metric, before, got):
    _, width, inner = mine.shape
    held = pl.BlockSpec(memory_space=pltpu.VMEM)
    return pl.pallas_call(
        rest_kernel,
        in_specs=[pl.BlockSpec(memory_space=pltpu.SMEM)] + [held] * 4,
        out_specs=[held] * 4,
        out_shape=[jax.ShapeDtypeStruct((width // 4, width), jnp.float32)] * 4,
        scratch_shapes=[pltpu.VMEM((width, inner), jnp.bfloat16)],
        compiler_params=pltpu.CompilerParams(vmem_limit_bytes=40 * 1024 * 1024),
        name="rest_exchange",
    )(place, mine, metric, before, got)


def double_metric(metric_inv):
    blocks = metric_inv.reshape(AUXB, 1, BLK, AUXB, 1, BLK)
    same = jnp.eye(2, dtype=jnp.bool_).reshape(1, 2, 1, 1, 2, 1)
    return jnp.where(same, blocks, 0).reshape(2 * NAUX, 2 * NAUX)


def part(table, index, axis):
    return lax.dynamic_index_in_dim(table, index, axis, keepdims=False)


def share_tags(tags, across, along):
    core, column, depth = lax.axis_index("c"), lax.axis_index("x"), lax.axis_index("z")
    swap = [(0, 1), (1, 0)]
    first = core == 0
    other = lax.ppermute(tags, "c", swap)
    both = jnp.where(first, jnp.stack([tags, other]), jnp.stack([other, tags])).reshape(2, across, along, 8)
    rows = [part(both, column, 1)]
    for away in range(1, across):
        steps = [(k, (k + away) % across) for k in range(across)]
        rows.append(lax.ppermute(part(both, (column + away) % across, 1), "x", steps))
    table = jnp.stack(rows)
    half = along // 2
    rows = []
    for away in range(1, half + 1):
        steps = [(z * 2 + c, (z + away + half * c) % along * 2 + c) for z in range(along) for c in range(2)]
        rows.append(lax.ppermute(part(table, (depth + away + half * core) % along, 2), ("z", "c"), steps))
    rows = jnp.stack(rows)
    return jnp.stack([rows, lax.ppermute(rows, "c", swap)])


def body(three_center, coefficients, metric_inv, target_owner, row_slot, aux_block, ao_block):
    orbitals = coefficients.shape[0]
    cores, across, along = lax.axis_size("c"), lax.axis_size("x"), lax.axis_size("z")
    main, extra, tags = make_units(
        three_center, coefficients, target_owner[:, 0], row_slot, aux_block, ao_block, (across, along)
    )
    devices = cores * across * 4 * along
    main = main.reshape(devices, MAIN, orbitals, LANES)
    extra = extra.reshape(devices, SLOTS - MAIN, orbitals, LANES)
    main = lax.all_to_all(main, AWAY, split_axis=0, concat_axis=0, tiled=True)
    metric = double_metric(metric_inv)

    tags = share_tags(tags, across, along).reshape(cores * across * along, 8)
    place = jnp.stack([lax.axis_index("c"), lax.axis_index("x"), lax.axis_index("z"), lax.axis_index("y")])

    def finish(tags, incoming, place, metric):
        incoming = [array.reshape(cores * across, 4, along, -1, orbitals, LANES) for array in incoming]
        mine, sent = gather_exchange(tags, place, incoming, metric)
        got = lax.ppermute(sent, "c", [(0, 1), (1, 0)])
        return tuple(rest_exchange(place, mine, metric, half_exchange(mine, metric), got))

    def few(main, extra, tags, place, metric):
        return finish(tags, [main], place, metric)

    def many(main, extra, tags, place, metric):
        extra = lax.all_to_all(extra, AWAY, split_axis=0, concat_axis=0, tiled=True)
        return finish(tags, [main, extra], place, metric)

    overflow = jnp.max(tags[:, SLOTS]) > MAIN
    shares = lax.cond(overflow, many, few, main, extra, tags, place, metric)
    total = shares[0]
    for away in (2, 1, 3):
        total += lax.ppermute(shares[away], "y", [(k, (k + away) % 4) for k in range(4)])
    return total.astype(jnp.bfloat16)


def solution(mesh):
    split = Mesh(mesh.devices.reshape(4, 8, 2, 4), AXES)
    pair = ("x", "z", "c")
    in_specs = (P(pair, "y", None), P(), P(), P(pair, None), P(pair), P(pair), P(pair))
    out_specs = P(AXES, None)
    return jax.shard_map(body, mesh=split, in_specs=in_specs, out_specs=out_specs, check_vma=False)
```

```python
import functools

import jax
import jax.numpy as jnp
from jax import lax
from jax.experimental import pallas as pl
from jax.experimental.pallas import tpu as pltpu
from jax.sharding import Mesh, PartitionSpec as P

BLK = 64
AUXB = 8
ROWB = 8
NAUX = 512
LANES = 128
SLOTS = 4
MAIN = 3
GROUP = 12
PARTS = 4
FETCH = 4
AXES = ("x", "z", "c", "y")
AWAY = ("c", "x", "y", "z")


def units_kernel(
    owner_ref, row_ref, aux_ref, ao_ref, three_ref, coef_ref,
    main_ref, extra_ref, tag_ref, rows_ref, made_ref, held_ref, spread_ref, chip_ref, slot_ref, got, sent
):
    count, _, depth_in = rows_ref.shape
    tiles = depth_in // LANES
    depth = tiles * 8
    orbitals = coef_ref.shape[0]
    chips, columns = tag_ref.shape
    depths = main_ref.shape[3]

    def fetch(step):
        units = pl.ds(step * FETCH, FETCH)
        return pltpu.make_async_copy(three_ref.at[units], rows_ref.at[units], got.at[step])

    orbitals_held = pltpu.make_async_copy(coef_ref, held_ref, got.at[count // FETCH])
    orbitals_held.start()

    def send(unit, act):
        chip, slot = chip_ref[unit], slot_ref[unit]
        across, along = chip // depths, chip % depths

        @pl.when(slot < MAIN)
        def _():
            act(pltpu.make_async_copy(made_ref.at[unit], main_ref.at[:, across, :, along, slot], sent.at[unit]))

        @pl.when(slot >= MAIN)
        def _():
            act(pltpu.make_async_copy(made_ref.at[unit], extra_ref.at[:, across, :, along, 0], sent.at[unit]))

    for step in range(count // FETCH):
        fetch(step).start()

    held = lax.broadcasted_iota(jnp.int32, (LANES, 2 * depth), 0)
    column = lax.broadcasted_iota(jnp.int32, (LANES, 2 * depth), 1)
    source = 2 * (column % depth // 8) + column // depth
    for half in range(2):
        spread_ref[half] = jnp.where(held == half * BLK + source, 1.0, 0.0).astype(jnp.bfloat16)

    def clear(chip, carry):
        for k in range(columns):
            tag_ref[chip, k] = -1 if k < SLOTS else 0
        return carry

    lax.fori_loop(0, chips, clear, 0)

    def rank(unit, fullest):
        owner = owner_ref[unit]
        chip = owner // 2
        slot = tag_ref[chip, SLOTS]
        chip_ref[unit] = chip
        slot_ref[unit] = slot
        tag_ref[chip, slot] = owner % 2 * (ROWB * AUXB) + row_ref[unit] * AUXB + aux_ref[unit]
        tag_ref[chip, SLOTS] = slot + 1
        return jnp.maximum(fullest, slot + 1)

    fullest = lax.fori_loop(0, count, rank, 0)

    def note(chip, carry):
        tag_ref[chip, SLOTS] = fullest
        return carry

    lax.fori_loop(0, chips, note, 0)

    lane = lax.broadcasted_iota(jnp.int32, (orbitals, 8, depth), 2)
    row = lax.broadcasted_iota(jnp.int32, (orbitals, 8, depth), 1)
    keep = (lane & 7) == row
    low = lax.broadcasted_iota(jnp.int32, (orbitals // 2, 8, LANES), 2) < BLK

    orbitals_held.wait()

    def group(step, carry):
        for k in range(GROUP // FETCH):
            fetch(step * (GROUP // FETCH) + k).wait()
        spreads = []
        for k in range(GROUP):
            ao = ao_ref[step * GROUP + k]
            picked = held_ref[:, pl.ds(pl.multiple_of(ao // 2 * LANES, LANES), LANES)]
            spreads.append(jnp.dot(picked, spread_ref[ao % 2], preferred_element_type=jnp.float32))
        for k in range(GROUP):
            rows = rows_ref[step * GROUP + k].astype(jnp.float32)
            stacked = [
                jnp.concatenate([rows[h * 8 : h * 8 + 8, j * LANES : (j + 1) * LANES] for j in range(tiles)], axis=0)
                for h in range(2)
            ]
            right = jnp.concatenate(stacked, axis=1).astype(jnp.bfloat16)
            parts = []
            for parity in range(2):
                wide = spreads[k][:, None, parity * depth : (parity + 1) * depth]
                wide = jnp.broadcast_to(wide, (orbitals, 8, depth))
                left = jnp.where(keep, wide, 0.0).reshape(orbitals * 8, depth).astype(jnp.bfloat16)
                made = jnp.dot(left, right, preferred_element_type=jnp.float32)
                parts.append(made.reshape(orbitals // 2, 2, 8, 2 * LANES))
            done = []
            for h in range(2):
                cut = slice(h * LANES, (h + 1) * LANES)
                stay = jnp.where(low, parts[0][:, 0, :, cut], parts[1][:, 1, :, cut])
                move = jnp.where(low, parts[0][:, 1, :, cut], parts[1][:, 0, :, cut])
                done.append(stay + pltpu.roll(move, BLK, 2))
            units = jnp.stack(done, axis=1).reshape(orbitals * 8, LANES).astype(jnp.bfloat16)
            made_ref[step * GROUP + k] = units.reshape(2, 4, orbitals, LANES)
        for k in range(GROUP):
            send(step * GROUP + k, lambda copy: copy.start())
        return carry

    lax.fori_loop(0, count // GROUP, group, 0)
    for unit in range(count):
        send(unit, lambda copy: copy.wait())


def make_units(three_center, coefficients, owner, row_slot, aux_block, ao_block, chips):
    count, rows, depth = three_center.shape
    orbitals = coefficients.shape[0]
    across, along = chips
    scalars = pl.BlockSpec(memory_space=pltpu.SMEM)
    main = (2, across, 4, along, MAIN, orbitals, LANES)
    extra = (2, across, 4, along, SLOTS - MAIN, orbitals, LANES)
    return pl.pallas_call(
        units_kernel,
        in_specs=[scalars] * 4
        + [pl.BlockSpec(memory_space=pltpu.HBM)] * 2,
        out_specs=[pl.BlockSpec(memory_space=pltpu.HBM)] * 2 + [scalars],
        out_shape=[
            jax.ShapeDtypeStruct(main, jnp.bfloat16),
            jax.ShapeDtypeStruct(extra, jnp.bfloat16),
            jax.ShapeDtypeStruct((across * along, 8), jnp.int32),
        ],
        scratch_shapes=[
            pltpu.VMEM((count, rows, depth), jnp.bfloat16),
            pltpu.VMEM((count, 2, 4, orbitals, LANES), jnp.bfloat16),
            pltpu.VMEM(coefficients.shape, jnp.bfloat16),
            pltpu.VMEM((2, LANES, BLK * 8), jnp.bfloat16),
            pltpu.SMEM((count,), jnp.int32),
            pltpu.SMEM((count,), jnp.int32),
            pltpu.SemaphoreType.DMA((count // FETCH + 1,)),
            pltpu.SemaphoreType.DMA((count,)),
        ],
        compiler_params=pltpu.CompilerParams(vmem_limit_bytes=60 * 1024 * 1024),
        name="units",
    )(owner, row_slot, aux_block, ao_block, three_center, coefficients)


def fit(whole, metric_ref, fitted):
    for orbital in range(2):
        cut = slice(orbital * NAUX, (orbital + 1) * NAUX)
        made = jnp.dot(whole[:, cut], metric_ref[...], preferred_element_type=jnp.float32)
        fitted[:, cut] = made.astype(jnp.bfloat16)


def own_exchange(whole, metric_ref, fitted, out_ref, first):
    fit(whole, metric_ref, fitted)
    part = lax.dot_general(fitted[...], whole, (((1,), (1,)), ((), ())), preferred_element_type=jnp.float32)
    if first:
        out_ref[...] = part
    else:
        out_ref[...] += part


def by_orbital(total, owner, pair):
    low = lax.broadcasted_iota(jnp.int32, total.shape[-2:], 1) < BLK
    lower, upper = [], []
    for aux in range(0, AUXB, 2):
        even, odd = total[owner, pair, aux], total[owner, pair, aux + 1]
        moved = pltpu.roll(jnp.where(low, odd, even), BLK, 1)
        lower.append(jnp.where(low, even, moved).astype(jnp.bfloat16))
        upper.append(jnp.where(low, moved, odd).astype(jnp.bfloat16))
    return lower + upper


def gather_kernel(tag_ref, place_ref, metric_ref, *refs):
    inputs = refs[: len(refs) - 6]
    mine_ref, out_ref, total, fitted, held, got = refs[len(refs) - 6 :]
    groups, quarters, depths, slots = held.shape[:4]
    columns = groups // 2
    planes = groups // PARTS

    def fetch(step):
        part = pl.ds(step * planes, planes)
        copies, first = [], 0
        for index, ref in enumerate(inputs):
            spots = pl.ds(first, ref.shape[3])
            copies.append(pltpu.make_async_copy(ref.at[part], held.at[part, :, :, spots], got.at[index, step]))
            first += ref.shape[3]
        return copies

    for step in range(PARTS):
        for copy in fetch(step):
            copy.start()
    total[...] = jnp.zeros_like(total)

    def add(source, carry):
        group, depth = lax.shift_right_logical(source, 3), source & (depths - 1)
        core, column = lax.shift_right_logical(group, 2), group & (columns - 1)
        away = (place_ref[2] - depth - 1) & (depths - 1)
        away = away ^ (place_ref[0] * (depths // 2))
        away = away * columns + ((place_ref[1] - column) & (columns - 1))
        for slot in range(slots):
            tag = tag_ref[away * 2 + core, slot]

            @pl.when(tag >= 0)
            def _():
                owner, row = lax.shift_right_logical(tag, 6), lax.shift_right_logical(tag, 3) & (ROWB - 1)
                aux = tag & (AUXB - 1)
                spots = [
                    (owner, pair, aux, pl.ds(pl.multiple_of(row * BLK + quarter * 16, 16), 16), slice(None))
                    for quarter in range(quarters)
                    for pair in range(2)
                ]
                news = [
                    held[group, quarter, depth, slot, pair * 16 : pair * 16 + 16, :].astype(jnp.float32)
                    for quarter in range(quarters)
                    for pair in range(2)
                ]
                sums = [total[spot] + new for spot, new in zip(spots, news)]
                for spot, value in zip(spots, sums):
                    total[spot] = value

        return carry

    for step in range(PARTS):
        for copy in fetch(step):
            copy.wait()
        lax.fori_loop(step * planes * depths, (step + 1) * planes * depths, add, 0)

    mine = place_ref[0]
    for pair in range(2):
        whole = jnp.concatenate(by_orbital(total, 1 - mine, pair), axis=1)
        own_exchange(whole, metric_ref, fitted, out_ref, pair == 0)
    for pair in range(2):
        for index, tile in enumerate(by_orbital(total, mine, pair)):
            mine_ref[pair, :, index * LANES : (index + 1) * LANES] = tile


def rest_kernel(place_ref, mine_ref, metric_ref, before_ref, got_ref, *refs):
    outs, fitted, made = refs[:-2], refs[-2], refs[-1]
    own_exchange(mine_ref[1], metric_ref, fitted, made, True)
    share = outs[0].shape[0]
    for away, out_ref in enumerate(outs):
        rows = pl.ds(pl.multiple_of(((place_ref[3] + away) & (len(outs) - 1)) * share, share), share)
        out_ref[...] = made[rows] + before_ref[rows] + got_ref[rows]


def half_kernel(mine_ref, metric_ref, out_ref, fitted):
    own_exchange(mine_ref[0], metric_ref, fitted, out_ref, True)


def gather_exchange(tags, place, incoming, metric):
    groups, quarters, depths, _, rows, lanes = incoming[0].shape
    slots = sum(array.shape[3] for array in incoming)
    width = ROWB * BLK
    inner = AUXB * lanes
    scalars = pl.BlockSpec(memory_space=pltpu.SMEM)
    held = pl.BlockSpec(memory_space=pltpu.VMEM)
    return pl.pallas_call(
        gather_kernel,
        in_specs=[scalars, scalars, held] + [pl.BlockSpec(memory_space=pltpu.HBM)] * len(incoming),
        out_specs=[held, held],
        out_shape=[
            jax.ShapeDtypeStruct((2, width, inner), jnp.bfloat16),
            jax.ShapeDtypeStruct((width, width), jnp.float32),
        ],
        scratch_shapes=[
            pltpu.VMEM((2, 2, AUXB, width, lanes), jnp.float32),
            pltpu.VMEM((width, inner), jnp.bfloat16),
            pltpu.VMEM((groups, quarters, depths, slots, rows, lanes), jnp.bfloat16),
            pltpu.SemaphoreType.DMA((len(incoming), PARTS)),
        ],
        compiler_params=pltpu.CompilerParams(vmem_limit_bytes=40 * 1024 * 1024),
        name="gather_exchange",
    )(tags, place, metric, *incoming)


def half_exchange(mine, metric):
    _, width, inner = mine.shape
    return pl.pallas_call(
        half_kernel,
        out_shape=jax.ShapeDtypeStruct((width, width), jnp.float32),
        scratch_shapes=[pltpu.VMEM((width, inner), jnp.bfloat16)],
        compiler_params=pltpu.CompilerParams(vmem_limit_bytes=40 * 1024 * 1024),
        cost_estimate=pl.CostEstimate(
            flops=2 * width * inner * (inner // 2 + width), bytes_accessed=5 * width * inner * 2, transcendentals=0
        ),
        name="half_exchange",
    )(mine, metric)


def rest_exchange(place, mine, metric, before, got):
    _, width, inner = mine.shape
    held = pl.BlockSpec(memory_space=pltpu.VMEM)
    return pl.pallas_call(
        rest_kernel,
        in_specs=[pl.BlockSpec(memory_space=pltpu.SMEM)] + [held] * 4,
        out_specs=[held] * 4,
        out_shape=[jax.ShapeDtypeStruct((width // 4, width), jnp.float32)] * 4,
        scratch_shapes=[pltpu.VMEM((width, inner), jnp.bfloat16), pltpu.VMEM((width, width), jnp.float32)],
        compiler_params=pltpu.CompilerParams(vmem_limit_bytes=40 * 1024 * 1024),
        name="rest_exchange",
    )(place, mine, metric, before, got)


def part(table, index, axis):
    return lax.dynamic_index_in_dim(table, index, axis, keepdims=False)


def share_tags(tags, across, along):
    core, column, depth = lax.axis_index("c"), lax.axis_index("x"), lax.axis_index("z")
    swap = [(0, 1), (1, 0)]
    first = core == 0
    other = lax.ppermute(tags, "c", swap)
    both = jnp.where(first, jnp.stack([tags, other]), jnp.stack([other, tags])).reshape(2, across, along, 8)
    rows = [part(both, column, 1)]
    for away in range(1, across):
        steps = [(k, (k + away) % across) for k in range(across)]
        rows.append(lax.ppermute(part(both, (column + away) % across, 1), "x", steps))
    table = jnp.stack(rows)
    half = along // 2
    rows = []
    for away in range(1, half + 1):
        steps = [(z * 2 + c, (z + away + half * c) % along * 2 + c) for z in range(along) for c in range(2)]
        rows.append(lax.ppermute(part(table, (depth + away + half * core) % along, 2), ("z", "c"), steps))
    rows = jnp.stack(rows)
    return jnp.stack([rows, lax.ppermute(rows, "c", swap)])


def body(three_center, coefficients, metric_inv, target_owner, row_slot, aux_block, ao_block):
    orbitals = coefficients.shape[0]
    cores, across, along = lax.axis_size("c"), lax.axis_size("x"), lax.axis_size("z")
    main, extra, tags = make_units(
        three_center, coefficients, target_owner[:, 0], row_slot, aux_block, ao_block, (across, along)
    )
    devices = cores * across * 4 * along
    main = main.reshape(devices, MAIN, orbitals, LANES)
    extra = extra.reshape(devices, SLOTS - MAIN, orbitals, LANES)
    main = lax.all_to_all(main, AWAY, split_axis=0, concat_axis=0, tiled=True)

    tags = share_tags(tags, across, along).reshape(cores * across * along, 8)
    place = jnp.stack([lax.axis_index("c"), lax.axis_index("x"), lax.axis_index("z"), lax.axis_index("y")])

    def finish(tags, incoming, place, metric):
        incoming = [array.reshape(cores * across, 4, along, -1, orbitals, LANES) for array in incoming]
        mine, sent = gather_exchange(tags, place, incoming, metric)
        got = lax.ppermute(sent, "c", [(0, 1), (1, 0)])
        return tuple(rest_exchange(place, mine, metric, half_exchange(mine, metric), got))

    def few(main, extra, tags, place, metric):
        return finish(tags, [main], place, metric)

    def many(main, extra, tags, place, metric):
        extra = lax.all_to_all(extra, AWAY, split_axis=0, concat_axis=0, tiled=True)
        return finish(tags, [main, extra], place, metric)

    overflow = jnp.max(tags[:, SLOTS]) > MAIN
    shares = lax.cond(overflow, many, few, main, extra, tags, place, metric_inv)
    total = shares[0]
    for away in (2, 1, 3):
        total += lax.ppermute(shares[away], "y", [(k, (k + away) % 4) for k in range(4)])
    return total.astype(jnp.bfloat16)


def solution(mesh):
    split = Mesh(mesh.devices.reshape(4, 8, 2, 4), AXES)
    pair = ("x", "z", "c")
    in_specs = (P(pair, "y", None), P(), P(), P(pair, None), P(pair), P(pair), P(pair))
    out_specs = P(AXES, None)
    return jax.shard_map(body, mesh=split, in_specs=in_specs, out_specs=out_specs, check_vma=False)
```

```python
import functools

import jax
import jax.numpy as jnp
from jax import lax
from jax.experimental import pallas as pl
from jax.experimental.pallas import tpu as pltpu
from jax.sharding import Mesh, PartitionSpec as P

BLK = 64
AUXB = 8
ROWB = 8
NAUX = 512
LANES = 128
SLOTS = 4
MAIN = 3
GROUP = 12
PARTS = 4
FETCH = 4
AXES = ("x", "z", "c", "y")
AWAY = ("c", "x", "y", "z")


def units_kernel(
    owner_ref, row_ref, aux_ref, ao_ref, three_ref, coef_ref,
    main_ref, extra_ref, tag_ref, rows_ref, made_ref, held_ref, spread_ref, chip_ref, slot_ref, got, sent
):
    count, _, depth_in = rows_ref.shape
    tiles = depth_in // LANES
    depth = tiles * 8
    orbitals = coef_ref.shape[0]
    chips, columns = tag_ref.shape
    depths = main_ref.shape[3]

    def fetch(step):
        units = pl.ds(step * FETCH, FETCH)
        return pltpu.make_async_copy(three_ref.at[units], rows_ref.at[units], got.at[step])

    orbitals_held = pltpu.make_async_copy(coef_ref, held_ref, got.at[count // FETCH])
    orbitals_held.start()

    def send(unit, act):
        chip, slot = chip_ref[unit], slot_ref[unit]
        across, along = chip // depths, chip % depths

        @pl.when(slot < MAIN)
        def _():
            act(pltpu.make_async_copy(made_ref.at[unit], main_ref.at[:, across, :, along, slot], sent.at[unit]))

        @pl.when(slot >= MAIN)
        def _():
            act(pltpu.make_async_copy(made_ref.at[unit], extra_ref.at[:, across, :, along, 0], sent.at[unit]))

    for step in range(count // FETCH):
        fetch(step).start()

    held = lax.broadcasted_iota(jnp.int32, (LANES, 2 * depth), 0)
    column = lax.broadcasted_iota(jnp.int32, (LANES, 2 * depth), 1)
    source = 2 * (column % depth // 8) + column // depth
    for half in range(2):
        spread_ref[half] = jnp.where(held == half * BLK + source, 1.0, 0.0).astype(jnp.bfloat16)

    def clear(chip, carry):
        for k in range(columns):
            tag_ref[chip, k] = -1 if k < SLOTS else 0
        return carry

    lax.fori_loop(0, chips, clear, 0)

    def rank(unit, fullest):
        owner = owner_ref[unit]
        chip = owner // 2
        slot = tag_ref[chip, SLOTS]
        chip_ref[unit] = chip
        slot_ref[unit] = slot
        tag_ref[chip, slot] = owner % 2 * (ROWB * AUXB) + row_ref[unit] * AUXB + aux_ref[unit]
        tag_ref[chip, SLOTS] = slot + 1
        return jnp.maximum(fullest, slot + 1)

    fullest = lax.fori_loop(0, count, rank, 0)

    def note(chip, carry):
        tag_ref[chip, SLOTS] = fullest
        return carry

    lax.fori_loop(0, chips, note, 0)

    lane = lax.broadcasted_iota(jnp.int32, (orbitals, 8, depth), 2)
    row = lax.broadcasted_iota(jnp.int32, (orbitals, 8, depth), 1)
    keep = (lane & 7) == row
    low = lax.broadcasted_iota(jnp.int32, (orbitals // 2, 8, LANES), 2) < BLK

    orbitals_held.wait()

    def group(step, carry):
        for k in range(GROUP // FETCH):
            fetch(step * (GROUP // FETCH) + k).wait()
        spreads = []
        for k in range(GROUP):
            ao = ao_ref[step * GROUP + k]
            picked = held_ref[:, pl.ds(pl.multiple_of(ao // 2 * LANES, LANES), LANES)]
            spreads.append(jnp.dot(picked, spread_ref[ao % 2], preferred_element_type=jnp.float32))
        for k in range(GROUP):
            rows = rows_ref[step * GROUP + k].astype(jnp.float32)
            stacked = [
                jnp.concatenate([rows[h * 8 : h * 8 + 8, j * LANES : (j + 1) * LANES] for j in range(tiles)], axis=0)
                for h in range(2)
            ]
            right = jnp.concatenate(stacked, axis=1).astype(jnp.bfloat16)
            parts = []
            for parity in range(2):
                wide = spreads[k][:, None, parity * depth : (parity + 1) * depth]
                wide = jnp.broadcast_to(wide, (orbitals, 8, depth))
                left = jnp.where(keep, wide, 0.0).reshape(orbitals * 8, depth).astype(jnp.bfloat16)
                made = jnp.dot(left, right, preferred_element_type=jnp.float32)
                parts.append(made.reshape(orbitals // 2, 2, 8, 2 * LANES))
            done = []
            for h in range(2):
                cut = slice(h * LANES, (h + 1) * LANES)
                stay = jnp.where(low, parts[0][:, 0, :, cut], parts[1][:, 1, :, cut])
                move = jnp.where(low, parts[0][:, 1, :, cut], parts[1][:, 0, :, cut])
                done.append(stay + pltpu.roll(move, BLK, 2))
            units = jnp.stack(done, axis=1).reshape(orbitals * 8, LANES).astype(jnp.bfloat16)
            made_ref[step * GROUP + k] = units.reshape(2, 4, orbitals, LANES)
        for k in range(GROUP):
            send(step * GROUP + k, lambda copy: copy.start())
        return carry

    lax.fori_loop(0, count // GROUP, group, 0)
    for unit in range(count):
        send(unit, lambda copy: copy.wait())


def make_units(three_center, coefficients, owner, row_slot, aux_block, ao_block, chips):
    count, rows, depth = three_center.shape
    orbitals = coefficients.shape[0]
    across, along = chips
    scalars = pl.BlockSpec(memory_space=pltpu.SMEM)
    main = (2, across, 4, along, MAIN, orbitals, LANES)
    extra = (2, across, 4, along, SLOTS - MAIN, orbitals, LANES)
    return pl.pallas_call(
        units_kernel,
        in_specs=[scalars] * 4
        + [pl.BlockSpec(memory_space=pltpu.HBM)] * 2,
        out_specs=[pl.BlockSpec(memory_space=pltpu.HBM)] * 2 + [scalars],
        out_shape=[
            jax.ShapeDtypeStruct(main, jnp.bfloat16),
            jax.ShapeDtypeStruct(extra, jnp.bfloat16),
            jax.ShapeDtypeStruct((across * along, 8), jnp.int32),
        ],
        scratch_shapes=[
            pltpu.VMEM((count, rows, depth), jnp.bfloat16),
            pltpu.VMEM((count, 2, 4, orbitals, LANES), jnp.bfloat16),
            pltpu.VMEM(coefficients.shape, jnp.bfloat16),
            pltpu.VMEM((2, LANES, BLK * 8), jnp.bfloat16),
            pltpu.SMEM((count,), jnp.int32),
            pltpu.SMEM((count,), jnp.int32),
            pltpu.SemaphoreType.DMA((count // FETCH + 1,)),
            pltpu.SemaphoreType.DMA((count,)),
        ],
        compiler_params=pltpu.CompilerParams(vmem_limit_bytes=60 * 1024 * 1024),
        name="units",
    )(owner, row_slot, aux_block, ao_block, three_center, coefficients)


def fit(whole, metric_ref, fitted):
    for orbital in range(2):
        cut = slice(orbital * NAUX, (orbital + 1) * NAUX)
        made = jnp.dot(whole[:, cut], metric_ref[...], preferred_element_type=jnp.float32)
        fitted[:, cut] = made.astype(jnp.bfloat16)


def own_exchange(whole, metric_ref, fitted, out_ref, first):
    fit(whole, metric_ref, fitted)
    part = lax.dot_general(fitted[...], whole, (((1,), (1,)), ((), ())), preferred_element_type=jnp.float32)
    if first:
        out_ref[...] = part
    else:
        out_ref[...] += part


def by_orbital(total, owner, pair):
    low = lax.broadcasted_iota(jnp.int32, total.shape[-2:], 1) < BLK
    lower, upper = [], []
    for aux in range(0, AUXB, 2):
        even, odd = total[owner, pair, aux], total[owner, pair, aux + 1]
        moved = pltpu.roll(jnp.where(low, odd, even), BLK, 1)
        lower.append(jnp.where(low, even, moved).astype(jnp.bfloat16))
        upper.append(jnp.where(low, moved, odd).astype(jnp.bfloat16))
    return lower + upper


def gather_kernel(tag_ref, place_ref, metric_ref, *refs):
    inputs = refs[: len(refs) - 6]
    mine_ref, out_ref, total, fitted, held, got = refs[len(refs) - 6 :]
    groups, quarters, depths, slots = held.shape[:4]
    columns = groups // 2
    planes = groups // PARTS

    def fetch(step):
        part = pl.ds(step * planes, planes)
        copies, first = [], 0
        for index, ref in enumerate(inputs):
            spots = pl.ds(first, ref.shape[3])
            copies.append(pltpu.make_async_copy(ref.at[part], held.at[part, :, :, spots], got.at[index, step]))
            first += ref.shape[3]
        return copies

    for step in range(PARTS):
        for copy in fetch(step):
            copy.start()
    total[...] = jnp.zeros_like(total)

    def add(source, carry):
        group, depth = lax.shift_right_logical(source, 3), source & (depths - 1)
        core, column = lax.shift_right_logical(group, 2), group & (columns - 1)
        away = (place_ref[2] - depth - 1) & (depths - 1)
        away = away ^ (place_ref[0] * (depths // 2))
        away = away * columns + ((place_ref[1] - column) & (columns - 1))
        for slot in range(slots):
            tag = tag_ref[away * 2 + core, slot]

            @pl.when(tag >= 0)
            def _():
                owner, row = lax.shift_right_logical(tag, 6), lax.shift_right_logical(tag, 3) & (ROWB - 1)
                aux = tag & (AUXB - 1)
                spots = [
                    (owner, pair, aux, pl.ds(pl.multiple_of(row * BLK + quarter * 16, 16), 16), slice(None))
                    for quarter in range(quarters)
                    for pair in range(2)
                ]
                news = [
                    held[group, quarter, depth, slot, pair * 16 : pair * 16 + 16, :].astype(jnp.float32)
                    for quarter in range(quarters)
                    for pair in range(2)
                ]
                sums = [total[spot] + new for spot, new in zip(spots, news)]
                for spot, value in zip(spots, sums):
                    total[spot] = value

        return carry

    for step in range(PARTS):
        for copy in fetch(step):
            copy.wait()
        lax.fori_loop(step * planes * depths, (step + 1) * planes * depths, add, 0)

    mine = place_ref[0]
    for pair in range(2):
        whole = jnp.concatenate(by_orbital(total, 1 - mine, pair), axis=1)
        own_exchange(whole, metric_ref, fitted, out_ref, pair == 0)
    for pair in range(2):
        for index, tile in enumerate(by_orbital(total, mine, pair)):
            mine_ref[pair, :, index * LANES : (index + 1) * LANES] = tile


def rest_kernel(place_ref, mine_ref, metric_ref, before_ref, got_ref, *refs):
    outs, fitted, made = refs[:-2], refs[-2], refs[-1]
    own_exchange(mine_ref[1], metric_ref, fitted, made, True)
    share = outs[0].shape[0]
    for away, out_ref in enumerate(outs):
        rows = pl.ds(pl.multiple_of(((place_ref[3] + away) & (len(outs) - 1)) * share, share), share)
        out_ref[...] = made[rows] + before_ref[rows] + got_ref[rows]


def half_kernel(mine_ref, metric_ref, out_ref, fitted):
    own_exchange(mine_ref[0], metric_ref, fitted, out_ref, True)


def gather_exchange(tags, place, incoming, metric):
    groups, quarters, depths, _, rows, lanes = incoming[0].shape
    slots = sum(array.shape[3] for array in incoming)
    width = ROWB * BLK
    inner = AUXB * lanes
    scalars = pl.BlockSpec(memory_space=pltpu.SMEM)
    held = pl.BlockSpec(memory_space=pltpu.VMEM)
    return pl.pallas_call(
        gather_kernel,
        in_specs=[scalars, scalars, held] + [pl.BlockSpec(memory_space=pltpu.HBM)] * len(incoming),
        out_specs=[held, held],
        out_shape=[
            jax.ShapeDtypeStruct((2, width, inner), jnp.bfloat16),
            jax.ShapeDtypeStruct((width, width), jnp.float32),
        ],
        scratch_shapes=[
            pltpu.VMEM((2, 2, AUXB, width, lanes), jnp.float32),
            pltpu.VMEM((width, inner), jnp.bfloat16),
            pltpu.VMEM((groups, quarters, depths, slots, rows, lanes), jnp.bfloat16),
            pltpu.SemaphoreType.DMA((len(incoming), PARTS)),
        ],
        compiler_params=pltpu.CompilerParams(vmem_limit_bytes=40 * 1024 * 1024),
        name="gather_exchange",
    )(tags, place, metric, *incoming)


def half_exchange(mine, metric):
    _, width, inner = mine.shape
    return pl.pallas_call(
        half_kernel,
        out_shape=jax.ShapeDtypeStruct((width, width), jnp.float32),
        scratch_shapes=[pltpu.VMEM((width, inner), jnp.bfloat16)],
        compiler_params=pltpu.CompilerParams(vmem_limit_bytes=40 * 1024 * 1024),
        cost_estimate=pl.CostEstimate(
            flops=2 * width * inner * (inner // 2 + width), bytes_accessed=5 * width * inner * 2, transcendentals=0
        ),
        name="half_exchange",
    )(mine, metric)


def rest_exchange(place, mine, metric, before, got):
    _, width, inner = mine.shape
    held = pl.BlockSpec(memory_space=pltpu.VMEM)
    return pl.pallas_call(
        rest_kernel,
        in_specs=[pl.BlockSpec(memory_space=pltpu.SMEM)] + [held] * 4,
        out_specs=[held] * 4,
        out_shape=[jax.ShapeDtypeStruct((width // 4, width), jnp.float32)] * 4,
        scratch_shapes=[pltpu.VMEM((width, inner), jnp.bfloat16), pltpu.VMEM((width, width), jnp.float32)],
        compiler_params=pltpu.CompilerParams(vmem_limit_bytes=40 * 1024 * 1024),
        name="rest_exchange",
    )(place, mine, metric, before, got)


def part(table, index, axis):
    return lax.dynamic_index_in_dim(table, index, axis, keepdims=False)


def share_tags(tags, across, along):
    core, column, depth = lax.axis_index("c"), lax.axis_index("x"), lax.axis_index("z")
    swap = [(0, 1), (1, 0)]
    first = core == 0
    other = lax.ppermute(tags, "c", swap)
    both = jnp.where(first, jnp.stack([tags, other]), jnp.stack([other, tags])).reshape(2, across, along, 8)
    rows = [part(both, column, 1)]
    for away in range(1, across):
        steps = [(k, (k + away) % across) for k in range(across)]
        rows.append(lax.ppermute(part(both, (column + away) % across, 1), "x", steps))
    table = jnp.stack(rows)
    half = along // 2
    rows = []
    for away in range(1, half + 1):
        steps = [(z * 2 + c, (z + away + half * c) % along * 2 + c) for z in range(along) for c in range(2)]
        rows.append(lax.ppermute(part(table, (depth + away + half * core) % along, 2), ("z", "c"), steps))
    rows = jnp.stack(rows)
    return jnp.stack([rows, lax.ppermute(rows, "c", swap)])


def body(three_center, coefficients, metric_inv, target_owner, row_slot, aux_block, ao_block):
    orbitals = coefficients.shape[0]
    cores, across, along = lax.axis_size("c"), lax.axis_size("x"), lax.axis_size("z")
    main, extra, tags = make_units(
        three_center, coefficients, target_owner[:, 0], row_slot, aux_block, ao_block, (across, along)
    )
    devices = cores * across * 4 * along
    main = main.reshape(devices, MAIN, orbitals, LANES)
    extra = extra.reshape(devices, SLOTS - MAIN, orbitals, LANES)
    main = lax.all_to_all(main, AWAY, split_axis=0, concat_axis=0, tiled=True)

    tags = share_tags(tags, across, along).reshape(cores * across * along, 8)
    place = jnp.stack([lax.axis_index("c"), lax.axis_index("x"), lax.axis_index("z"), lax.axis_index("y")])

    def finish(tags, incoming, place, metric):
        incoming = [array.reshape(cores * across, 4, along, -1, orbitals, LANES) for array in incoming]
        mine, sent = gather_exchange(tags, place, incoming, metric)
        got = lax.ppermute(sent, "c", [(0, 1), (1, 0)])
        return tuple(rest_exchange(place, mine, metric, half_exchange(mine, metric), got))

    def few(main, extra, tags, place, metric):
        return finish(tags, [main], place, metric)

    def many(main, extra, tags, place, metric):
        extra = lax.all_to_all(extra, AWAY, split_axis=0, concat_axis=0, tiled=True)
        return finish(tags, [main, extra], place, metric)

    overflow = jnp.max(tags[:, SLOTS]) > MAIN
    shares = lax.cond(overflow, many, few, main, extra, tags, place, metric_inv)
    own, right, far, left = shares
    half = far.shape[0] // 2
    up, down = [(k, (k + 1) % 4) for k in range(4)], [(k, (k + 3) % 4) for k in range(4)]
    from_left, from_right = lax.ppermute(far[:half], "y", up), lax.ppermute(far[half:], "y", down)
    right = jnp.concatenate([right[:half] + from_left, right[half:]])
    left = jnp.concatenate([left[:half], left[half:] + from_right])
    return (own + lax.ppermute(right, "y", up) + lax.ppermute(left, "y", down)).astype(jnp.bfloat16)


def solution(mesh):
    split = Mesh(mesh.devices.reshape(4, 8, 2, 4), AXES)
    pair = ("x", "z", "c")
    in_specs = (P(pair, "y", None), P(), P(), P(pair, None), P(pair), P(pair), P(pair))
    out_specs = P(AXES, None)
    return jax.shard_map(body, mesh=split, in_specs=in_specs, out_specs=out_specs, check_vma=False)
```
